256 devices in a mesh: dp: 32 (over x, z_hi, core), tensor: 8 (over y, z_lo).
Axes of the slice: x: 4, y: 4, z: 8 (z_hi: 4, z_lo: 2; z = z_hi * 2 + z_lo), core: 2. Of those that a mesh axis runs over, the one named last changes fastest.
Arguments:
- tokens: bfloat16 [1280, 4096], P(('dp', 'tensor')), may hold values from -6 to 6
- cotangent: bfloat16 [1280, 4096], P(('dp', 'tensor')), may hold values from -6 to 6
- gate_weight: bfloat16 [4096, 16384], P('tensor', 'dp'), may hold values from -0.09375 to 0.09375
- up_weight: bfloat16 [4096, 16384], P('tensor', 'dp'), may hold values from -0.09375 to 0.09375
- down_weight: bfloat16 [16384, 4096], P('dp', 'tensor'), may hold values from -0.046875 to 0.046875
- probe_gate: bfloat16 [4096, 16384], P('tensor', 'dp'), may hold values from -6 to 6
- probe_up: bfloat16 [4096, 16384], P('tensor', 'dp'), may hold values from -6 to 6
- probe_down: bfloat16 [16384, 4096], P('dp', 'tensor'), may hold values from -6 to 6
- hess_gate: float32 [4096, 16384], P('tensor', 'dp'), may hold values from 0.05 to 2
- hess_up: float32 [4096, 16384], P('tensor', 'dp'), may hold values from 0.05 to 2
- hess_down: float32 [16384, 4096], P('dp', 'tensor'), may hold values from 0.05 to 2
- moment_gate: bfloat16 [4096, 16384], P('tensor', 'dp'), may hold values from -0.125 to 0.125
- moment_up: bfloat16 [4096, 16384], P('tensor', 'dp'), may hold values from -0.125 to 0.125
- moment_down: bfloat16 [16384, 4096], P('dp', 'tensor'), may hold values from -0.125 to 0.125
Outputs:
- new_hess_gate: float32 [4096, 16384], P('tensor', 'dp')
- new_hess_up: float32 [4096, 16384], P('tensor', 'dp')
- new_hess_down: float32 [16384, 4096], P('dp', 'tensor')
- step_gate: bfloat16 [4096, 16384], P('tensor', 'dp')
- step_up: bfloat16 [4096, 16384], P('tensor', 'dp')
- step_down: bfloat16 [16384, 4096], P('dp', 'tensor')
The draws below stay inside these ranges and needn't reach their ends.
All inputs are finite; a program needn't handle non-finite values.
Results may differ from the reference program's by a relative error of at most 0.0095.
Values may be sent and summed in bfloat16 or wider, within the bound.
A program may use at most 128 MiB of HBM per device.

```python
import math
import jax
import jax.numpy as jnp
from jax import lax

D = 4096
FF = 16384
TOKENS = 1280
N_TENSOR = 8


def block_scale(rng, extent, split, smallest, largest):
    def one(dim, parts):
        steps = jax.random.uniform(jax.random.fold_in(jax.random.fold_in(rng, 6), dim), (parts,), jnp.float32, smallest / len(split), largest / len(split))
        return jnp.repeat(jnp.exp(steps), extent[dim] // parts).reshape((-1,) + (1,) * (len(extent) - dim - 1))

    level = one(*split[0])
    for cut in split[1:]:
        level = level * one(*cut)
    return level


def centred(rng, dims, width, most, pieces=(), kind=jnp.bfloat16):
    level = block_scale(rng, dims, pieces, -0.22, 0.18) if pieces else 1.0
    array = jax.random.normal(rng, dims, jnp.float32) * width * level
    return jnp.minimum(jnp.maximum(array, -most), most).astype(kind)


def setup_inputs(seed: int = 0) -> dict:
    keys = jax.random.split(jax.random.key(seed), 15)
    return {
        "tokens": centred(keys[0], (TOKENS, D), 1.0, 6.0, ((0, 256),)),
        "cotangent": centred(keys[1], (TOKENS, D), 1.0, 6.0, ((0, 256),)),
        "gate_weight": centred(keys[2], (D, FF), D ** -0.5, 0.09375, ((0, 8), (1, 32))),
        "up_weight": centred(keys[3], (D, FF), D ** -0.5, 0.09375, ((0, 8), (1, 32))),
        "down_weight": centred(keys[4], (FF, D), FF ** -0.5, 0.046875, ((0, 32), (1, 8))),
        "probe_gate": centred(keys[5], (D, FF), 1.0, 6.0, ((0, 8), (1, 32))),
        "probe_up": centred(keys[6], (D, FF), 1.0, 6.0, ((0, 8), (1, 32))),
        "probe_down": centred(keys[7], (FF, D), 1.0, 6.0, ((0, 32), (1, 8))),
        "hess_gate": jnp.clip(jnp.exp(math.log(2.0) - 3.6888794 * jax.random.uniform(keys[8], (D, FF), jnp.float32) ** block_scale(keys[8], (D, FF), ((0, 8), (1, 32)), -0.2, 0.2)), 0.05, 2.0),
        "hess_up": jnp.clip(jnp.exp(math.log(2.0) - 3.6888794 * jax.random.uniform(keys[9], (D, FF), jnp.float32) ** block_scale(keys[9], (D, FF), ((0, 8), (1, 32)), -0.2, 0.2)), 0.05, 2.0),
        "hess_down": jnp.clip(jnp.exp(math.log(2.0) - 3.6888794 * jax.random.uniform(keys[10], (FF, D), jnp.float32) ** block_scale(keys[10], (FF, D), ((0, 32), (1, 8)), -0.2, 0.2)), 0.05, 2.0),
        "moment_gate": centred(keys[11], (D, FF), 0.02, 0.125, ((0, 8), (1, 32))),
        "moment_up": centred(keys[12], (D, FF), 0.02, 0.125, ((0, 8), (1, 32))),
        "moment_down": centred(keys[13], (FF, D), 0.02, 0.125, ((0, 32), (1, 8))),
    }


decay_rate = 0.9
curvature_scale = 0.05
floor_value = 0.01


def block_sum(rows_data, weights, transpose):
    feature_width = D // N_TENSOR
    total = jnp.zeros((rows_data.shape[0], FF), jnp.float32)
    for column in range(N_TENSOR):
        lower = column * feature_width
        upper = lower + feature_width
        piece_rows = rows_data[:, lower:upper]
        if transpose:
            partial_prod = jnp.dot(piece_rows, weights[:, lower:upper].T, preferred_element_type=jnp.float32)
        else:
            partial_prod = jnp.dot(piece_rows, weights[lower:upper, :], preferred_element_type=jnp.float32)
        rounded = lax.optimization_barrier(partial_prod.astype(jnp.bfloat16))
        total = total + rounded.astype(jnp.float32)
    return total


def tangent_terms(gate_pre, up_pre, back, gate_tan, up_tan, back_tan):
    logistic = jax.nn.sigmoid(gate_pre)
    activation = gate_pre * logistic
    first_deriv = logistic * (1.0 + gate_pre * (1.0 - logistic))
    second_deriv = logistic * (1.0 - logistic) * (2.0 + gate_pre * (1.0 - 2.0 * logistic))
    tan_gate_back = back_tan * up_pre * first_deriv + back * up_tan * first_deriv + back * up_pre * second_deriv * gate_tan
    tan_up_back = back_tan * activation + back * first_deriv * gate_tan
    tan_hidden = first_deriv * gate_tan * up_pre + activation * up_tan
    return tan_gate_back.astype(jnp.bfloat16), tan_up_back.astype(jnp.bfloat16), tan_hidden.astype(jnp.bfloat16)


def sophia_update(hess_prev, probe, product, moment):
    new_hess = decay_rate * hess_prev + (1.0 - decay_rate) * probe.astype(jnp.float32) * product
    ratio = moment.astype(jnp.float32) / jnp.maximum(curvature_scale * new_hess, floor_value)
    return new_hess, jnp.clip(ratio, -1.0, 1.0).astype(jnp.bfloat16)


def reference(tokens, cotangent, gate_weight, up_weight, down_weight, probe_gate, probe_up, probe_down, hess_gate, hess_up, hess_down, moment_gate, moment_up, moment_down):
    gate_pre = block_sum(tokens, gate_weight, False)
    up_pre = block_sum(tokens, up_weight, False)
    back = block_sum(cotangent, down_weight, True)
    gate_tan = block_sum(tokens, probe_gate, False)
    up_tan = block_sum(tokens, probe_up, False)
    back_tan = block_sum(cotangent, probe_down, True)
    tan_gate_back, tan_up_back, tan_hidden = tangent_terms(gate_pre, up_pre, back, gate_tan, up_tan, back_tan)
    product_gate = jnp.dot(tokens.T, tan_gate_back, preferred_element_type=jnp.float32) / TOKENS
    product_up = jnp.dot(tokens.T, tan_up_back, preferred_element_type=jnp.float32) / TOKENS
    product_down = jnp.dot(tan_hidden.T, cotangent, preferred_element_type=jnp.float32) / TOKENS
    new_hess_gate, step_gate = sophia_update(hess_gate, probe_gate, product_gate, moment_gate)
    new_hess_up, step_up = sophia_update(hess_up, probe_up, product_up, moment_up)
    new_hess_down, step_down = sophia_update(hess_down, probe_down, product_down, moment_down)
    return new_hess_gate, new_hess_up, new_hess_down, step_gate, step_up, step_down
```

```python
import jax
import jax.numpy as jnp
import numpy as np
from jax import lax
from jax.experimental import pallas as pl
from jax.experimental.pallas import tpu as pltpu
from jax.sharding import PartitionSpec as P

decay_rate = 0.9
curvature_scale = 0.05
floor_value = 0.01

MESH = pl.DeviceIdType.MESH
ANY = pl.BlockSpec(memory_space=pl.ANY)
VMEM = pl.BlockSpec(memory_space=pltpu.VMEM)
DMA = pltpu.SemaphoreType.DMA

NX, NY, NZ = 4, 4, 4
ROWS = 5
GROUP = 80
FEAT = 512
WIDE = NY * FEAT
TOKENS = 1280
SUB = 128


def place():
    d = lax.axis_index("dp")
    t = lax.axis_index("tensor")
    return d // 8, t // 2, (d // 2) % 4, t % 2, d % 2


def device(x, y, zh, zl, c):
    return {"dp": x * 8 + zh * 2 + c, "tensor": y * 2 + zl}


def remote(src, dst, send, recv, target):
    return pltpu.make_async_remote_copy(
        src_ref=src, dst_ref=dst, send_sem=send, recv_sem=recv,
        device_id=target, device_id_type=MESH,
    )


def enter(targets):
    barrier = pltpu.get_barrier_semaphore()
    for target in targets:
        pl.semaphore_signal(barrier, inc=1, device_id=target, device_id_type=MESH)
    pl.semaphore_wait(barrier, len(targets))


def gather_kernel(
    tok_ref, cot_ref, pick_ref, gate_ref, up_ref, pgate_ref, pup_ref, down_ref, pdown_ref,
    all_ref, wide_ref, tall_ref,
    packed32, packed, pieces, block,
    ps, pr, ws, wr, wl, zs, zr, xs, xr, ss, sr, own_sem,
):
    x, y, zh, zl, c = place()
    group = [(dc, dy, dz) for dc in range(2) for dy in range(4) for dz in range(2)][1:]
    mates = [((y + dy) % 4, zl ^ dz, c ^ dc) for dc, dy, dz in group]
    sib = device(x, y, zh, zl, 1 - c)
    zn, zp = device(x, y, (zh + 1) % 4, zl, c), device(x, y, (zh + 3) % 4, zl, c)
    xn, xp = device((x + 1) % 4, y, zh, zl, c), device((x + 3) % 4, y, zh, zl, c)
    enter([device(x, my, zh, mz, mc) for my, mz, mc in mates] + [zn, zp, xn, xp])

    for arr, ref in enumerate((tok_ref, cot_ref)):
        for mz in range(2):
            packed32[...] = jnp.zeros_like(packed32)
            for my in range(4):
                col = (my * 2 + mz) * FEAT
                packed32[8 * (my // 2):8 * (my // 2) + ROWS, (my % 2) * FEAT:(my % 2 + 1) * FEAT] = (
                    ref[:, col:col + FEAT].astype(jnp.float32)
                )
            packed[mz, arr] = packed32[...].astype(jnp.bfloat16)
    me = c * 8 + y * 2 + zl
    piece_copies = []
    for k, (my, mz, mc) in enumerate(mates):
        cp = remote(packed.at[mz, mc], pieces.at[me], ps.at[k], pr.at[k], device(x, my, zh, mz, mc))
        cp.start()
        piece_copies.append(cp)
    pieces[me] = packed[zl, c]

    weight_copies = []
    col_refs = (gate_ref, up_ref, pgate_ref, pup_ref)
    row_refs = (down_ref, pdown_ref)

    def cut(k, to):
        if k < 4:
            return (
                col_refs[k].at[:, pl.ds(pl.multiple_of(to * SUB, SUB), SUB)],
                wide_ref.at[pl.ds(pl.multiple_of(y * FEAT, FEAT), FEAT), pl.ds(k * SUB, SUB)],
            )
        return (
            row_refs[k - 4].at[pl.ds(pl.multiple_of(to * SUB, SUB), SUB), :],
            tall_ref.at[pl.ds((k - 4) * SUB, SUB), pl.ds(pl.multiple_of(y * FEAT, FEAT), FEAT)],
        )

    for k in range(6):
        for dy in (1, 3, 2):
            to = (y + dy) % 4
            src, dst = cut(k, to)
            cp = remote(src, dst, ws.at[dy - 1, k], wr.at[dy - 1, k], device(x, to, zh, zl, c))
            cp.start()
            weight_copies.append(cp)
        src, dst = cut(k, y)
        cp = pltpu.make_async_copy(src, dst, wl.at[k])
        cp.start()
        weight_copies.append(cp)

    for cp in piece_copies:
        cp.wait_recv()
    spread = pieces[...].reshape(256, 1024)
    for half in range(2):
        block[:, half * 1024:(half + 1) * 1024] = jnp.dot(
            pick_ref[half], spread, preferred_element_type=jnp.float32
        ).astype(jnp.bfloat16)

    HALF = WIDE // 2
    zrel = (0, 3, 1, 2)
    sends = []
    pending = {}

    def where(dx, k, half=None):
        g = ((x + dx) % 4) * 4 + (zh + zrel[k]) % 4
        rows = pl.ds(pl.multiple_of(g * GROUP, 16), GROUP)
        if half is None:
            return all_ref.at[c, rows, :]
        return all_ref.at[c, rows, pl.ds(half * HALF, HALF)]

    def go(src, dst, s, r, target):
        cp = remote(src, dst, s, r, target)
        cp.start()
        sends.append(cp)

    def arrive(dst, s, r):
        remote(dst, dst, s, r, sib).wait_recv()

    def share(dx, k, src=None):
        ref = where(dx, k)
        n = dx * 4 + k
        go(ref if src is None else src, ref, ss.at[n], sr.at[n], sib)

    def along_x(k, src=None):
        ref = where(0, k)
        src = ref if src is None else src
        go(src, ref, xs.at[0, k], xr.at[0, k], xn)
        go(src, ref, xs.at[1, k], xr.at[1, k], xp)

    def pass_x(k):
        arrive(where(3, k), xs.at[0, k], xr.at[0, k])
        half = where(3, k, 0)
        go(half, half, xs.at[2, k], xr.at[2, k], xn)
        arrive(where(1, k), xs.at[1, k], xr.at[1, k])
        half = where(1, k, 1)
        go(half, half, xs.at[3, k], xr.at[3, k], xp)
        share(3, k)
        share(1, k)

    def end_x(k):
        arrive(where(2, k, 0), xs.at[2, k], xr.at[2, k])
        arrive(where(2, k, 1), xs.at[3, k], xr.at[3, k])
        share(2, k)

    here = where(0, 0)
    go(block, here, zs.at[0], zr.at[0], zn)
    go(block, here, zs.at[1], zr.at[1], zp)
    along_x(0, block)
    share(0, 0, block)
    keep = pltpu.make_async_copy(block, here, own_sem)
    keep.start()
    pass_x(0)
    arrive(where(0, 1), zs.at[0], zr.at[0])
    half = where(0, 1, 0)
    go(half, half, zs.at[2], zr.at[2], zn)
    arrive(where(0, 2), zs.at[1], zr.at[1])
    half = where(0, 2, 1)
    go(half, half, zs.at[3], zr.at[3], zp)
    along_x(1)
    along_x(2)
    share(0, 1)
    share(0, 2)
    end_x(0)
    arrive(where(0, 3, 0), zs.at[2], zr.at[2])
    arrive(where(0, 3, 1), zs.at[3], zr.at[3])
    along_x(3)
    share(0, 3)
    pass_x(1)
    pass_x(2)
    end_x(1)
    end_x(2)
    pass_x(3)
    end_x(3)
    for cp in weight_copies:
        cp.wait()
    keep.wait()
    for cp in piece_copies:
        cp.wait_send()
    for cp in sends:
        cp.wait_send()
    for dx in range(4):
        for k in range(4):
            g = ((x + dx) % 4) * 4 + (zh + zrel[k]) % 4
            ref = all_ref.at[1 - c, pl.ds(pl.multiple_of(g * GROUP, 16), GROUP), :]
            arrive(ref, ss.at[dx * 4 + k], sr.at[dx * 4 + k])


def gather(tokens, cotangent, gate, up, pgate, pup, down, pdown):
    pick = np.zeros((2, GROUP, 256), np.float32)
    for half in range(2):
        for row in range(GROUP):
            pick[half, row, 16 * (row // ROWS) + row % ROWS + 8 * half] = 1.0
    bf = jnp.bfloat16
    return pl.pallas_call(
        gather_kernel,
        out_shape=(
            jax.ShapeDtypeStruct((2, TOKENS, WIDE), bf),
            jax.ShapeDtypeStruct((WIDE, 4 * SUB), bf),
            jax.ShapeDtypeStruct((2 * SUB, WIDE), bf),
        ),
        in_specs=[VMEM] * 3 + [ANY] * 6,
        out_specs=(ANY, ANY, ANY),
        scratch_shapes=[
            pltpu.VMEM((16, 1024), jnp.float32),
            pltpu.VMEM((2, 2, 16, 1024), bf),
            pltpu.VMEM((16, 16, 1024), bf),
            pltpu.VMEM((GROUP, WIDE), bf),
            DMA((15,)), DMA((15,)),
            DMA((3, 6)), DMA((3, 6)), DMA((6,)),
            DMA((4,)), DMA((4,)),
            DMA((4, 4)), DMA((4, 4)),
            DMA((16,)), DMA((16,)),
            DMA(()),
        ],
        compiler_params=pltpu.CompilerParams(
            collective_id=0, has_side_effects=True, vmem_limit_bytes=40 << 20
        ),
    )(tokens, cotangent, jnp.asarray(pick, bf), gate, up, pgate, pup, down, pdown)


CHUNKS = 4
CHUNK = TOKENS // 2 // CHUNKS


def tangent_kernel(sums_ref, back_ref, out_ref, far_sums, far_back, s1, r1, s2, r2, s3, r3):
    x, y, zh, zl, c = place()
    mate = device(x, y, zh, 1 - zl, c)
    enter([mate])
    copies = []
    for k in range(CHUNKS):
        rows = pl.ds(pl.multiple_of((1 - zl) * (TOKENS // 2) + k * CHUNK, 16), CHUNK)
        a = remote(sums_ref.at[rows, :], far_sums.at[k], s1.at[k], r1.at[k], mate)
        b = remote(back_ref.at[rows, :], far_back.at[k], s2.at[k], r2.at[k], mate)
        a.start()
        b.start()
        copies.append((a, b))
    outs = []
    for k in range(CHUNKS):
        for cp in copies[k]:
            cp.wait_recv()
        rows = pl.ds(pl.multiple_of(zl * (TOKENS // 2) + k * CHUNK, 16), CHUNK)

        def total(near, far, n):
            cols = slice(n * SUB, (n + 1) * SUB)
            return near[rows, cols].astype(jnp.float32) + far[k, :, cols].astype(jnp.float32)

        gate_pre, up_pre, gate_tan, up_tan = (total(sums_ref, far_sums, n) for n in range(4))
        back, back_tan = (total(back_ref, far_back, n) for n in range(2))
        logistic = 1.0 / (1.0 + jnp.exp(-gate_pre))
        activation = gate_pre * logistic
        first = logistic * (1.0 + gate_pre * (1.0 - logistic))
        second = logistic * (1.0 - logistic) * (2.0 + gate_pre * (1.0 - 2.0 * logistic))
        out_ref[rows, 0:SUB] = (
            back_tan * up_pre * first + back * up_tan * first + back * up_pre * second * gate_tan
        ).astype(jnp.bfloat16)
        out_ref[rows, SUB:2 * SUB] = (back_tan * activation + back * first * gate_tan).astype(jnp.bfloat16)
        out_ref[rows, 2 * SUB:] = (first * gate_tan * up_pre + activation * up_tan).astype(jnp.bfloat16)
        cp = remote(out_ref.at[rows, :], out_ref.at[rows, :], s3.at[k], r3.at[k], mate)
        cp.start()
        outs.append(cp)
    for k in range(CHUNKS):
        rows = pl.ds(pl.multiple_of((1 - zl) * (TOKENS // 2) + k * CHUNK, 16), CHUNK)
        remote(out_ref.at[rows, :], out_ref.at[rows, :], s3.at[k], r3.at[k], mate).wait_recv()
        for cp in copies[k]:
            cp.wait_send()
        outs[k].wait_send()


def tangents(sums, back):
    bf = jnp.bfloat16
    return pl.pallas_call(
        tangent_kernel,
        out_shape=jax.ShapeDtypeStruct((TOKENS, 3 * SUB), bf),
        in_specs=[VMEM] * 2,
        out_specs=VMEM,
        scratch_shapes=[
            pltpu.VMEM((CHUNKS, CHUNK, 4 * SUB), bf),
            pltpu.VMEM((CHUNKS, CHUNK, 2 * SUB), bf),
        ] + [DMA((CHUNKS,))] * 6,
        compiler_params=pltpu.CompilerParams(
            collective_id=1, has_side_effects=True, vmem_limit_bytes=40 << 20
        ),
    )(sums, back)


def return_kernel(wide_ref, tall_ref, gate_ref, up_ref, down_ref, send, recv, local_sem):
    x, y, zh, zl, c = place()
    enter([device(x, (y + dy) % 4, zh, zl, c) for dy in (1, 2, 3)])

    def cut(k, to):
        feats = pl.ds(pl.multiple_of(to * FEAT, FEAT), FEAT)
        mine = pl.ds(pl.multiple_of(y * SUB, SUB), SUB)
        if k < 2:
            return wide_ref.at[feats, pl.ds(k * SUB, SUB)], (gate_ref, up_ref)[k].at[:, mine]
        return tall_ref.at[:, feats], down_ref.at[mine, :]

    copies = []
    for k in range(3):
        for dy in (1, 3, 2):
            to = (y + dy) % 4
            src, dst = cut(k, to)
            cp = remote(src, dst, send.at[dy - 1, k], recv.at[dy - 1, k], device(x, to, zh, zl, c))
            cp.start()
            copies.append(cp)
        src, dst = cut(k, y)
        cp = pltpu.make_async_copy(src, dst, local_sem.at[k])
        cp.start()
        copies.append(cp)
    for cp in copies:
        cp.wait()


def give_back(wide, tall):
    bf = jnp.bfloat16
    return pl.pallas_call(
        return_kernel,
        out_shape=(jax.ShapeDtypeStruct((FEAT, 4 * SUB), bf),) * 2 + (jax.ShapeDtypeStruct((4 * SUB, FEAT), bf),),
        in_specs=[VMEM] * 2,
        out_specs=(VMEM,) * 3,
        scratch_shapes=[DMA((3, 3)), DMA((3, 3)), DMA((3,))],
        compiler_params=pltpu.CompilerParams(
            collective_id=2, has_side_effects=True, vmem_limit_bytes=40 << 20
        ),
    )(wide, tall)


def sophia_update(hess_prev, probe, product, moment):
    new_hess = decay_rate * hess_prev + (1.0 - decay_rate) * probe.astype(jnp.float32) * product.astype(jnp.float32)
    ratio = moment.astype(jnp.float32) / jnp.maximum(curvature_scale * new_hess, floor_value)
    return new_hess, jnp.clip(ratio, -1.0, 1.0).astype(jnp.bfloat16)


def local(
    tokens, cotangent, gate_weight, up_weight, down_weight, probe_gate, probe_up, probe_down,
    hess_gate, hess_up, hess_down, moment_gate, moment_up, moment_down,
):
    every, wide, tall = gather(
        tokens, cotangent, gate_weight, up_weight, probe_gate, probe_up, down_weight, probe_down
    )
    toks, cots = every[0], every[1]
    f32, bf = jnp.float32, jnp.bfloat16
    sums = jnp.dot(toks, wide, preferred_element_type=f32).astype(bf)
    back = lax.dot_general(cots, tall, (((1,), (1,)), ((), ())), preferred_element_type=f32).astype(bf)
    tans = tangents(sums, back)
    wide_out = lax.dot_general(toks, tans[:, :2 * SUB], (((0,), (0,)), ((), ())), preferred_element_type=f32)
    tall_out = lax.dot_general(tans[:, 2 * SUB:], cots, (((0,), (0,)), ((), ())), preferred_element_type=f32)
    products = give_back((wide_out / TOKENS).astype(bf), (tall_out / TOKENS).astype(bf))
    new_hess_gate, step_gate = sophia_update(hess_gate, probe_gate, products[0], moment_gate)
    new_hess_up, step_up = sophia_update(hess_up, probe_up, products[1], moment_up)
    new_hess_down, step_down = sophia_update(hess_down, probe_down, products[2], moment_down)
    return new_hess_gate, new_hess_up, new_hess_down, step_gate, step_up, step_down


def solution(mesh):
    cols, rows, split = P("tensor", "dp"), P("dp", "tensor"), P(("dp", "tensor"), None)
    per = (cols, cols, rows)
    return jax.shard_map(
        local, mesh=mesh,
        in_specs=(split, split) + per * 4,
        out_specs=per * 2,
        check_vma=False,
    )
```

```python
import jax
import jax.numpy as jnp
import numpy as np
from jax import lax
from jax.experimental import pallas as pl
from jax.experimental.pallas import tpu as pltpu
from jax.sharding import PartitionSpec as P

decay_rate = 0.9
curvature_scale = 0.05
floor_value = 0.01

MESH = pl.DeviceIdType.MESH
ANY = pl.BlockSpec(memory_space=pl.ANY)
VMEM = pl.BlockSpec(memory_space=pltpu.VMEM)
DMA = pltpu.SemaphoreType.DMA

NX, NY, NZ = 4, 4, 4
ROWS = 5
GROUP = 80
FEAT = 512
WIDE = NY * FEAT
TOKENS = 1280
SUB = 128


def place():
    d = lax.axis_index("dp")
    t = lax.axis_index("tensor")
    return d // 8, t // 2, (d // 2) % 4, t % 2, d % 2


def device(x, y, zh, zl, c):
    return {"dp": x * 8 + zh * 2 + c, "tensor": y * 2 + zl}


def remote(src, dst, send, recv, target):
    return pltpu.make_async_remote_copy(
        src_ref=src, dst_ref=dst, send_sem=send, recv_sem=recv,
        device_id=target, device_id_type=MESH,
    )


def enter(targets):
    barrier = pltpu.get_barrier_semaphore()
    for target in targets:
        pl.semaphore_signal(barrier, inc=1, device_id=target, device_id_type=MESH)
    pl.semaphore_wait(barrier, len(targets))

HALF = WIDE // 2
SPAN = TOKENS // NX
OWN = SPAN // 2
ZREL = (0, 3, 1, 2)


def refresh_kernel(
    tok_ref, cot_ref, pick_ref, gate_ref, up_ref, pgate_ref, pup_ref, down_ref, pdown_ref,
    gate_out, up_out, down_out,
    packed32, packed, pieces, every, wide, tall, part, far, tans, back_wide, back_tall,
    ps, pr, ws, wr, wl, zs, zr, xs, xr, ss, sr, rs, rr, ts, tr, os, orr, ol,
):
    x, y, zh, zl, c = place()
    f32, bf = jnp.float32, jnp.bfloat16
    group = [(dc, dy, dz) for dc in range(2) for dy in range(4) for dz in range(2)][1:]
    mates = [((y + dy) % 4, zl ^ dz, c ^ dc) for dc, dy, dz in group]
    sib = device(x, y, zh, zl, 1 - c)
    pair = device(x, y, zh, 1 - zl, c)
    zn, zp = device(x, y, (zh + 1) % 4, zl, c), device(x, y, (zh + 3) % 4, zl, c)
    xn, xp = device((x + 1) % 4, y, zh, zl, c), device((x + 3) % 4, y, zh, zl, c)
    enter([device(x, my, zh, mz, mc) for my, mz, mc in mates] + [zn, zp, xn, xp])

    for arr, ref in enumerate((tok_ref, cot_ref)):
        for mz in range(2):
            packed32[...] = jnp.zeros_like(packed32)
            for my in range(4):
                col = (my * 2 + mz) * FEAT
                packed32[8 * (my // 2):8 * (my // 2) + ROWS, (my % 2) * FEAT:(my % 2 + 1) * FEAT] = (
                    ref[:, col:col + FEAT].astype(f32)
                )
            packed[mz, arr] = packed32[...].astype(bf)
    me = c * 8 + y * 2 + zl
    piece_copies = []
    for k, (my, mz, mc) in enumerate(mates):
        cp = remote(packed.at[mz, mc], pieces.at[me], ps.at[k], pr.at[k], device(x, my, zh, mz, mc))
        cp.start()
        piece_copies.append(cp)
    pieces[me] = packed[zl, c]

    weight_copies = []
    col_refs = (gate_ref, up_ref, pgate_ref, pup_ref)
    row_refs = (down_ref, pdown_ref)

    def cut(k, to):
        if k < 4:
            return (
                col_refs[k].at[:, pl.ds(pl.multiple_of(to * SUB, SUB), SUB)],
                wide.at[pl.ds(pl.multiple_of(y * FEAT, FEAT), FEAT), pl.ds(k * SUB, SUB)],
            )
        return (
            row_refs[k - 4].at[pl.ds(pl.multiple_of(to * SUB, SUB), SUB), :],
            tall.at[pl.ds((k - 4) * SUB, SUB), pl.ds(pl.multiple_of(y * FEAT, FEAT), FEAT)],
        )

    for k in range(6):
        for dy in (1, 3, 2):
            to = (y + dy) % 4
            src, dst = cut(k, to)
            cp = remote(src, dst, ws.at[dy - 1, k], wr.at[dy - 1, k], device(x, to, zh, zl, c))
            cp.start()
            weight_copies.append(cp)
        src, dst = cut(k, y)
        cp = pltpu.make_async_copy(src, dst, wl.at[k])
        cp.start()
        weight_copies.append(cp)

    sends = []

    def rows_of(dx, k):
        g = ((x + dx) % 4) * 4 + (zh + ZREL[k]) % 4
        return pl.ds(pl.multiple_of(g * GROUP, 16), GROUP)

    def where(dx, k, half=None):
        if half is None:
            return every.at[c, rows_of(dx, k), :]
        return every.at[c, rows_of(dx, k), pl.ds(half * HALF, HALF)]

    def go(src, dst, s, r, target):
        cp = remote(src, dst, s, r, target)
        cp.start()
        sends.append(cp)

    def arrive(dst, s, r):
        remote(dst, dst, s, r, sib).wait_recv()

    def share(dx, k):
        ref = where(dx, k)
        go(ref, ref, ss.at[dx * 4 + k], sr.at[dx * 4 + k], sib)

    def shared(dx):
        for k in range(4):
            arrive(every.at[1 - c, rows_of(dx, k), :], ss.at[dx * 4 + k], sr.at[dx * 4 + k])

    def along_x(k):
        ref = where(0, k)
        go(ref, ref, xs.at[0, k], xr.at[0, k], xn)
        go(ref, ref, xs.at[1, k], xr.at[1, k], xp)

    def pass_x(k):
        arrive(where(3, k), xs.at[0, k], xr.at[0, k])
        half = where(3, k, 0)
        go(half, half, xs.at[2, k], xr.at[2, k], xn)
        arrive(where(1, k), xs.at[1, k], xr.at[1, k])
        half = where(1, k, 1)
        go(half, half, xs.at[3, k], xr.at[3, k], xp)
        share(3, k)
        share(1, k)

    def end_x(k):
        arrive(where(2, k, 0), xs.at[2, k], xr.at[2, k])
        arrive(where(2, k, 1), xs.at[3, k], xr.at[3, k])
        share(2, k)

    def span(dx):
        return ((x + dx) % 4) * SPAN

    def partial(dx):
        rows = pl.ds(pl.multiple_of(span(dx), 16), SPAN)
        part[rows, 0:4 * SUB] = jnp.dot(every[0, rows, :], wide[...], preferred_element_type=f32).astype(bf)
        part[rows, 4 * SUB:] = lax.dot_general(
            every[1, rows, :], tall[...], (((1,), (1,)), ((), ())), preferred_element_type=f32
        ).astype(bf)
        theirs = pl.ds(pl.multiple_of(span(dx) + (1 - zl) * OWN, 16), OWN)
        go(part.at[theirs, :], far.at[dx], rs.at[dx], rr.at[dx], pair)

    def tangent(dx):
        arrive(far.at[dx], rs.at[dx], rr.at[dx])
        rows = pl.ds(pl.multiple_of(span(dx) + zl * OWN, 16), OWN)

        def total(n):
            cols = slice(n * SUB, (n + 1) * SUB)
            return part[rows, cols].astype(f32) + far[dx, :, cols].astype(f32)

        gate_pre, up_pre, gate_tan, up_tan, back, back_tan = (total(n) for n in range(6))
        logistic = 1.0 / (1.0 + jnp.exp(-gate_pre))
        activation = gate_pre * logistic
        first = logistic * (1.0 + gate_pre * (1.0 - logistic))
        second = logistic * (1.0 - logistic) * (2.0 + gate_pre * (1.0 - 2.0 * logistic))
        tans[rows, 0:SUB] = (
            back_tan * up_pre * first + back * up_tan * first + back * up_pre * second * gate_tan
        ).astype(bf)
        tans[rows, SUB:2 * SUB] = (back_tan * activation + back * first * gate_tan).astype(bf)
        tans[rows, 2 * SUB:] = (first * gate_tan * up_pre + activation * up_tan).astype(bf)
        go(tans.at[rows, :], tans.at[rows, :], ts.at[dx], tr.at[dx], pair)

    def tangent_there(dx):
        rows = pl.ds(pl.multiple_of(span(dx) + (1 - zl) * OWN, 16), OWN)
        arrive(tans.at[rows, :], ts.at[dx], tr.at[dx])

    g = x * 4 + zh
    for cp in piece_copies:
        cp.wait_recv()
    spread = pieces[...].reshape(256, 1024)
    for half in range(2):
        every[c, rows_of(0, 0), half * HALF:(half + 1) * HALF] = jnp.dot(
            pick_ref[half], spread, preferred_element_type=f32
        ).astype(bf)
    here = where(0, 0)
    go(here, here, zs.at[0], zr.at[0], zn)
    go(here, here, zs.at[1], zr.at[1], zp)
    along_x(0)
    share(0, 0)
    pass_x(0)
    arrive(where(0, 1), zs.at[0], zr.at[0])
    half = where(0, 1, 0)
    go(half, half, zs.at[2], zr.at[2], zn)
    arrive(where(0, 2), zs.at[1], zr.at[1])
    half = where(0, 2, 1)
    go(half, half, zs.at[3], zr.at[3], zp)
    along_x(1)
    along_x(2)
    share(0, 1)
    share(0, 2)
    end_x(0)
    arrive(where(0, 3, 0), zs.at[2], zr.at[2])
    arrive(where(0, 3, 1), zs.at[3], zr.at[3])
    along_x(3)
    share(0, 3)
    pass_x(1)
    pass_x(2)
    for cp in weight_copies:
        cp.wait()
    shared(0)
    partial(0)
    pass_x(3)
    end_x(1)
    end_x(2)
    shared(3)
    partial(3)
    shared(1)
    partial(1)
    tangent(0)
    end_x(3)
    tangent(3)
    shared(2)
    partial(2)
    tangent(1)
    tangent(2)
    for dx in (0, 3, 1, 2):
        tangent_there(dx)

    out_copies = []
    mine = pl.ds(pl.multiple_of(y * SUB, SUB), SUB)
    for dy in (2, 1, 3, 0):
        to = (y + dy) % 4
        feats = pl.ds(pl.multiple_of(to * FEAT, FEAT), FEAT)
        both = lax.dot_general(
            tans[:, 0:2 * SUB], every[0, :, feats], (((0,), (0,)), ((), ())), preferred_element_type=f32
        ) * (1.0 / TOKENS)
        back_wide[feats, :] = both.T.astype(bf)
        back_tall[:, feats] = (lax.dot_general(
            tans[:, 2 * SUB:], every[1, :, feats], (((0,), (0,)), ((), ())), preferred_element_type=f32
        ) * (1.0 / TOKENS)).astype(bf)
        pairs = (
            (back_wide.at[feats, pl.ds(0, SUB)], gate_out.at[:, mine]),
            (back_wide.at[feats, pl.ds(SUB, SUB)], up_out.at[:, mine]),
            (back_tall.at[:, feats], down_out.at[mine, :]),
        )
        for k, (src, dst) in enumerate(pairs):
            if dy:
                cp = remote(src, dst, os.at[dy - 1, k], orr.at[dy - 1, k], device(x, to, zh, zl, c))
            else:
                cp = pltpu.make_async_copy(src, dst, ol.at[k])
            cp.start()
            out_copies.append(cp)
    for cp in out_copies:
        cp.wait()
    for cp in piece_copies:
        cp.wait_send()
    for cp in sends:
        cp.wait_send()


def products_of(tokens, cotangent, gate, up, pgate, pup, down, pdown):
    pick = np.zeros((2, GROUP, 256), np.float32)
    for half in range(2):
        for row in range(GROUP):
            pick[half, row, 16 * (row // ROWS) + row % ROWS + 8 * half] = 1.0
    bf = jnp.bfloat16
    return pl.pallas_call(
        refresh_kernel,
        out_shape=(jax.ShapeDtypeStruct((FEAT, 4 * SUB), bf),) * 2 + (jax.ShapeDtypeStruct((4 * SUB, FEAT), bf),),
        in_specs=[VMEM] * 3 + [ANY] * 6,
        out_specs=(ANY, ANY, ANY),
        scratch_shapes=[
            pltpu.VMEM((16, 1024), jnp.float32),
            pltpu.VMEM((2, 2, 16, 1024), bf),
            pltpu.VMEM((16, 16, 1024), bf),
            pltpu.VMEM((2, TOKENS, WIDE), bf),
            pltpu.VMEM((WIDE, 4 * SUB), bf),
            pltpu.VMEM((2 * SUB, WIDE), bf),
            pltpu.VMEM((TOKENS, 6 * SUB), bf),
            pltpu.VMEM((NX, OWN, 6 * SUB), bf),
            pltpu.VMEM((TOKENS, 3 * SUB), bf),
            pltpu.VMEM((WIDE, 2 * SUB), bf),
            pltpu.VMEM((SUB, WIDE), bf),
            DMA((15,)), DMA((15,)),
            DMA((3, 6)), DMA((3, 6)), DMA((6,)),
            DMA((4,)), DMA((4,)),
            DMA((4, 4)), DMA((4, 4)),
            DMA((16,)), DMA((16,)),
            DMA((NX,)), DMA((NX,)), DMA((NX,)), DMA((NX,)),
            DMA((3, 3)), DMA((3, 3)), DMA((3,)),
        ],
        compiler_params=pltpu.CompilerParams(
            collective_id=0, has_side_effects=True, vmem_limit_bytes=60 << 20
        ),
    )(tokens, cotangent, jnp.asarray(pick, bf), gate, up, pgate, pup, down, pdown)


def sophia_update(hess_prev, probe, product, moment):
    new_hess = decay_rate * hess_prev + (1.0 - decay_rate) * probe.astype(jnp.float32) * product.astype(jnp.float32)
    ratio = moment.astype(jnp.float32) / jnp.maximum(curvature_scale * new_hess, floor_value)
    return new_hess, jnp.clip(ratio, -1.0, 1.0).astype(jnp.bfloat16)


def local(
    tokens, cotangent, gate_weight, up_weight, down_weight, probe_gate, probe_up, probe_down,
    hess_gate, hess_up, hess_down, moment_gate, moment_up, moment_down,
):
    products = products_of(
        tokens, cotangent, gate_weight, up_weight, probe_gate, probe_up, down_weight, probe_down
    )
    new_hess_gate, step_gate = sophia_update(hess_gate, probe_gate, products[0], moment_gate)
    new_hess_up, step_up = sophia_update(hess_up, probe_up, products[1], moment_up)
    new_hess_down, step_down = sophia_update(hess_down, probe_down, products[2], moment_down)
    return new_hess_gate, new_hess_up, new_hess_down, step_gate, step_up, step_down


def solution(mesh):
    cols, rows, split = P("tensor", "dp"), P("dp", "tensor"), P(("dp", "tensor"), None)
    per = (cols, cols, rows)
    return jax.shard_map(
        local, mesh=mesh,
        in_specs=(split, split) + per * 4,
        out_specs=per * 2,
        check_vma=False,
    )
```

```python
import jax
import jax.numpy as jnp
import numpy as np
from jax import lax
from jax.experimental import pallas as pl
from jax.experimental.pallas import tpu as pltpu
from jax.sharding import PartitionSpec as P

decay_rate = 0.9
curvature_scale = 0.05
floor_value = 0.01

MESH = pl.DeviceIdType.MESH
ANY = pl.BlockSpec(memory_space=pl.ANY)
VMEM = pl.BlockSpec(memory_space=pltpu.VMEM)
DMA = pltpu.SemaphoreType.DMA

NX, NY, NZ = 4, 4, 4
ROWS = 5
GROUP = 80
FEAT = 512
WIDE = NY * FEAT
TOKENS = 1280
SUB = 128


def place():
    d = lax.axis_index("dp")
    t = lax.axis_index("tensor")
    return d // 8, t // 2, (d // 2) % 4, t % 2, d % 2


def device(x, y, zh, zl, c):
    return {"dp": x * 8 + zh * 2 + c, "tensor": y * 2 + zl}


def remote(src, dst, send, recv, target):
    return pltpu.make_async_remote_copy(
        src_ref=src, dst_ref=dst, send_sem=send, recv_sem=recv,
        device_id=target, device_id_type=MESH,
    )

LANE = WIDE // 2
HALF = LANE // 2
RUN = 768
SPAN = TOKENS // NZ
OWN = SPAN // 2
ZREL = (0, 3, 1, 2)
TOK, COT = 0, 1


def refresh_kernel(
    tok_ref, cot_ref, pick_ref, gate_ref, up_ref, pgate_ref, pup_ref, down_ref, pdown_ref,
    gate_out, up_out, down_out,
    packed32, packed, pieces, every, wide, tall, part_t, part_c, far_t, far_c, tan_h, tan_gu, back_wide, back_tall,
    ps, pr, ws, wr, wl, zs, zr, xs, xr, ss, sr, rs, rr, ts, tr, os, orr, ol,
):
    x, y, zh, zl, c = place()
    f32, bf = jnp.float32, jnp.bfloat16
    group = [(dc, dy, dz) for dc in range(2) for dy in range(4) for dz in range(2)][1:]
    mates = [((y + dy) % 4, zl ^ dz, c ^ dc) for dc, dy, dz in group]
    sib = device(x, y, zh, zl, 1 - c)
    pair = device(x, y, zh, 1 - zl, c)
    zn, zp = device(x, y, (zh + 1) % 4, zl, c), device(x, y, (zh + 3) % 4, zl, c)
    xn, xp = device((x + 1) % 4, y, zh, zl, c), device((x + 3) % 4, y, zh, zl, c)
    barrier = pltpu.get_barrier_semaphore()
    friends = [device(x, my, zh, mz, mc) for my, mz, mc in mates] + [zn, zp, xn, xp]
    for friend in friends:
        pl.semaphore_signal(barrier, inc=1, device_id=friend, device_id_type=MESH)

    packed32[...] = jnp.zeros_like(packed32)
    for mz in range(2):
        for mc in range(2):
            for n in range(8):
                ref = (tok_ref, cot_ref)[n // 4]
                col = ((2 * mc + n % 4 // 2) * 2 + mz) * FEAT + n % 2 * 256
                row, at = n // 3 * ROWS, n % 3 * 256
                packed32[row:row + ROWS, at:at + 256] = ref[:, col:col + 256].astype(f32)
            packed[mz, mc] = packed32[...].astype(bf)
    pl.semaphore_wait(barrier, len(friends))
    me = c * 8 + y * 2 + zl
    piece_copies = []
    for k, (my, mz, mc) in enumerate(mates):
        cp = remote(packed.at[mz, mc], pieces.at[me], ps.at[k], pr.at[k], device(x, my, zh, mz, mc))
        cp.start()
        piece_copies.append(cp)
    pieces[me] = packed[zl, c]

    weight_copies = []
    col_refs = (gate_ref, up_ref, pgate_ref, pup_ref)
    row_refs = (down_ref, pdown_ref)

    def cut(k, to):
        if k < 4:
            return (
                col_refs[k].at[:, pl.ds(pl.multiple_of(to * SUB, SUB), SUB)],
                wide.at[pl.ds(pl.multiple_of(y * FEAT, FEAT), FEAT), pl.ds(k * SUB, SUB)],
            )
        return (
            row_refs[k - 4].at[pl.ds(pl.multiple_of(to * SUB, SUB), SUB), :],
            tall.at[pl.ds((k - 4) * SUB, SUB), pl.ds(pl.multiple_of(y * FEAT, FEAT), FEAT)],
        )

    def lend(kinds):
        for k in kinds:
            for dy in (1, 3, 2):
                to = (y + dy) % 4
                src, dst = cut(k, to)
                cp = remote(src, dst, ws.at[dy - 1, k], wr.at[dy - 1, k], device(x, to, zh, zl, c))
                cp.start()
                weight_copies.append(cp)
            src, dst = cut(k, y)
            cp = pltpu.make_async_copy(src, dst, wl.at[k])
            cp.start()
            weight_copies.append(cp)

    sends = []

    def where(arr, dx, k, half=None):
        g = ((zh + ZREL[k]) % 4) * 4 + (x + dx) % 4
        rows = pl.ds(pl.multiple_of(g * GROUP, 16), GROUP)
        if half is None:
            return every.at[arr, rows, pl.ds(pl.multiple_of(c * LANE, LANE), LANE)]
        return every.at[arr, rows, pl.ds(pl.multiple_of(c * LANE + half * HALF, HALF), HALF)]

    def go(src, dst, s, r, target):
        cp = remote(src, dst, s, r, target)
        cp.start()
        sends.append(cp)

    def arrive(dst, s, r):
        remote(dst, dst, s, r, sib).wait_recv()

    def share(a, dx, k):
        ref = where(a, dx, k)
        go(ref, ref, ss.at[a, dx, k], sr.at[a, dx, k], sib)

    def shared(a, k):
        for dx in range(4):
            g = ((zh + ZREL[k]) % 4) * 4 + (x + dx) % 4
            rows = pl.ds(pl.multiple_of(g * GROUP, 16), GROUP)
            ref = every.at[a, rows, pl.ds(pl.multiple_of((1 - c) * LANE, LANE), LANE)]
            arrive(ref, ss.at[a, dx, k], sr.at[a, dx, k])

    def z_send(a, way, half):
        ref = where(a, 0, 0, half)
        cp = remote(ref, ref, zs.at[a, way, half], zr.at[a, way, half], (zn, zp)[way])
        cp.start()
        return cp

    def z_get(a, way, half):
        ref = where(a, 0, 1 + way, half)
        arrive(ref, zs.at[a, way, half], zr.at[a, way, half])
        if half == way:
            go(ref, ref, zs.at[a, way, 2], zr.at[a, way, 2], (zn, zp)[way])
        x_send(a, 1 + way, half)

    def z_end(a):
        for way in range(2):
            arrive(where(a, 0, 3, way), zs.at[a, way, 2], zr.at[a, way, 2])
            x_send(a, 3, way)
        share(a, 0, 3)

    def x_send(a, k, half):
        ref = where(a, 0, k, half)
        for way in (half, 1 - half):
            go(ref, ref, xs.at[a, way, k, half], xr.at[a, way, k, half], (xn, xp)[way])

    def x_get(a, way, k, half):
        ref = where(a, (3, 1)[way], k, half)
        arrive(ref, xs.at[a, way, k, half], xr.at[a, way, k, half])
        if half == way:
            go(ref, ref, xs.at[a, way, k, 2], xr.at[a, way, k, 2], (xn, xp)[way])

    def x_share(a, k):
        share(a, 3, k)
        share(a, 1, k)

    def x_end(a, k):
        for way in range(2):
            arrive(where(a, 2, k, way), xs.at[a, way, k, 2], xr.at[a, way, k, 2])
        share(a, 2, k)

    def span(k):
        return ((zh + ZREL[k]) % 4) * SPAN

    def rows_of(k):
        return pl.ds(pl.multiple_of(span(k), 16), SPAN)

    def near(k):
        return pl.ds(pl.multiple_of(span(k) + zl * OWN, 16), OWN)

    def away(k):
        return pl.ds(pl.multiple_of(span(k) + (1 - zl) * OWN, 16), OWN)

    def sum_t(k):
        shared(TOK, k)
        part_t[rows_of(k), :] = jnp.dot(every[TOK, rows_of(k), :], wide[...], preferred_element_type=f32).astype(bf)
        go(part_t.at[away(k), :], far_t.at[k], rs.at[0, k], rr.at[0, k], pair)

    def sum_c(k):
        shared(COT, k)
        part_c[rows_of(k), :] = lax.dot_general(
            every[COT, rows_of(k), :], tall[...], (((1,), (1,)), ((), ())), preferred_element_type=f32
        ).astype(bf)
        go(part_c.at[away(k), :], far_c.at[k], rs.at[1, k], rr.at[1, k], pair)

    def total_t(k, n):
        cols = slice(n * SUB, (n + 1) * SUB)
        return part_t[near(k), cols].astype(f32) + far_t[k, :, cols].astype(f32)

    def total_c(k, n):
        cols = slice(n * SUB, (n + 1) * SUB)
        return part_c[near(k), cols].astype(f32) + far_c[k, :, cols].astype(f32)

    def hidden(k):
        arrive(far_t.at[k], rs.at[0, k], rr.at[0, k])
        gate_pre, up_pre, gate_tan, up_tan = (total_t(k, n) for n in range(4))
        logistic = 1.0 / (1.0 + jnp.exp(-gate_pre))
        first = logistic * (1.0 + gate_pre * (1.0 - logistic))
        tan_h[near(k), :] = (first * gate_tan * up_pre + gate_pre * logistic * up_tan).astype(bf)
        ref = tan_h.at[near(k), :]
        go(ref, ref, ts.at[0, k], tr.at[0, k], pair)

    def tangent(k):
        arrive(far_c.at[k], rs.at[1, k], rr.at[1, k])
        gate_pre, up_pre, gate_tan, up_tan = (total_t(k, n) for n in range(4))
        back, back_tan = (total_c(k, n) for n in range(2))
        logistic = 1.0 / (1.0 + jnp.exp(-gate_pre))
        first = logistic * (1.0 + gate_pre * (1.0 - logistic))
        second = logistic * (1.0 - logistic) * (2.0 + gate_pre * (1.0 - 2.0 * logistic))
        tan_gu[near(k), 0:SUB] = (
            back_tan * up_pre * first + back * up_tan * first + back * up_pre * second * gate_tan
        ).astype(bf)
        tan_gu[near(k), SUB:] = (back_tan * gate_pre * logistic + back * first * gate_tan).astype(bf)
        ref = tan_gu.at[near(k), :]
        go(ref, ref, ts.at[1, k], tr.at[1, k], pair)

    def there(ref, n, k):
        ref = ref.at[away(k), :]
        arrive(ref, ts.at[n, k], tr.at[n, k])

    out_copies = []
    mine = pl.ds(pl.multiple_of(y * SUB, SUB), SUB)

    def give(dy, pairs):
        to = (y + dy) % 4
        for k, src, dst in pairs:
            if dy:
                cp = remote(src, dst, os.at[dy - 1, k], orr.at[dy - 1, k], device(x, to, zh, zl, c))
            else:
                cp = pltpu.make_async_copy(src, dst, ol.at[k])
            cp.start()
            out_copies.append(cp)

    def feats_of(dy):
        return pl.ds(pl.multiple_of(((y + dy) % 4) * FEAT, FEAT), FEAT)

    def product_down(dy):
        feats = feats_of(dy)
        back_tall[:, feats] = (lax.dot_general(
            tan_h[...], every[COT, :, feats], (((0,), (0,)), ((), ())), preferred_element_type=f32
        ) * (1.0 / TOKENS)).astype(bf)
        give(dy, [(2, back_tall.at[:, feats], down_out.at[mine, :])])

    def product_wide(dy):
        feats = feats_of(dy)
        both = lax.dot_general(
            tan_gu[...], every[TOK, :, feats], (((0,), (0,)), ((), ())), preferred_element_type=f32
        ) * (1.0 / TOKENS)
        back_wide[feats, :] = both.T.astype(bf)
        give(dy, [
            (0, back_wide.at[feats, pl.ds(0, SUB)], gate_out.at[:, mine]),
            (1, back_wide.at[feats, pl.ds(SUB, SUB)], up_out.at[:, mine]),
        ])

    for cp in piece_copies:
        cp.wait_recv()
    spread = pieces[...].reshape(256, RUN)
    block = jnp.concatenate([
        jnp.dot(pick_ref[n], spread[:, :min(RUN, WIDE - n * RUN)], preferred_element_type=f32).astype(bf)
        for n in range(3)
    ], axis=1)
    for arr in (TOK, COT):
        where(arr, 0, 0)[...] = block[:, arr * LANE:(arr + 1) * LANE]

    t_first = [z_send(TOK, 0, 0), z_send(TOK, 1, 1)]
    x_send(TOK, 0, 0)
    x_send(TOK, 0, 1)
    share(TOK, 0, 0)
    lend(range(6))
    for cp in t_first:
        cp.wait_send()
    sends.append(z_send(TOK, 0, 1))
    sends.append(z_send(TOK, 1, 0))
    x_get(TOK, 0, 0, 0)
    x_get(TOK, 1, 0, 1)
    z_get(TOK, 0, 0)
    z_get(TOK, 1, 1)
    x_get(TOK, 0, 0, 1)
    x_get(TOK, 1, 0, 0)
    x_share(TOK, 0)
    c_first = [z_send(COT, 0, 0), z_send(COT, 1, 1)]
    x_send(COT, 0, 0)
    x_send(COT, 0, 1)
    share(COT, 0, 0)
    z_get(TOK, 0, 1)
    z_get(TOK, 1, 0)
    share(TOK, 0, 1)
    share(TOK, 0, 2)
    x_end(TOK, 0)
    z_end(TOK)
    for cp in c_first:
        cp.wait_send()
    sends.append(z_send(COT, 0, 1))
    sends.append(z_send(COT, 1, 0))
    x_get(TOK, 0, 1, 0)
    x_get(TOK, 1, 2, 1)
    x_get(TOK, 1, 1, 1)
    x_get(TOK, 0, 2, 0)
    x_get(COT, 0, 0, 0)
    x_get(COT, 1, 0, 1)
    z_get(COT, 0, 0)
    z_get(COT, 1, 1)
    x_get(TOK, 1, 1, 0)
    x_get(TOK, 0, 2, 1)
    x_get(TOK, 0, 1, 1)
    x_get(TOK, 1, 2, 0)
    x_share(TOK, 1)
    x_share(TOK, 2)
    x_get(COT, 0, 0, 1)
    x_get(COT, 1, 0, 0)
    x_share(COT, 0)
    z_get(COT, 0, 1)
    z_get(COT, 1, 0)
    share(COT, 0, 1)
    share(COT, 0, 2)
    x_end(TOK, 1)
    x_end(TOK, 2)
    x_get(TOK, 0, 3, 0)
    x_get(TOK, 1, 3, 1)
    x_get(TOK, 0, 3, 1)
    x_get(TOK, 1, 3, 0)
    x_share(TOK, 3)
    z_end(COT)
    for cp in weight_copies[:16]:
        cp.wait()
    sum_t(0)
    x_end(COT, 0)
    x_get(COT, 0, 1, 0)
    x_get(COT, 1, 2, 1)
    sum_t(1)
    x_end(TOK, 3)
    sum_t(2)
    x_get(COT, 1, 1, 1)
    x_get(COT, 0, 2, 0)
    sum_t(3)
    x_get(COT, 1, 1, 0)
    x_get(COT, 0, 2, 1)
    x_get(COT, 0, 1, 1)
    x_get(COT, 1, 2, 0)
    x_share(COT, 1)
    x_share(COT, 2)
    hidden(0)
    for cp in weight_copies[16:]:
        cp.wait()
    sum_c(0)
    hidden(1)
    x_get(COT, 0, 3, 0)
    x_get(COT, 1, 3, 1)
    x_end(COT, 1)
    x_end(COT, 2)
    sum_c(1)
    hidden(2)
    x_get(COT, 0, 3, 1)
    x_get(COT, 1, 3, 0)
    x_share(COT, 3)
    sum_c(2)
    hidden(3)
    tangent(0)
    x_end(COT, 3)
    tangent(1)
    tangent(2)
    sum_c(3)
    for k in range(4):
        there(tan_h, 0, k)
    product_down(2)
    product_down(1)
    product_down(3)
    tangent(3)
    product_down(0)
    for k in range(4):
        there(tan_gu, 1, k)
    for dy in (2, 1, 3, 0):
        product_wide(dy)
    for cp in out_copies:
        cp.wait()
    for cp in piece_copies:
        cp.wait_send()
    for cp in sends:
        cp.wait_send()


def products_of(tokens, cotangent, gate, up, pgate, pup, down, pdown):
    pick = np.zeros((3, GROUP, 256), np.float32)
    for n in range(3):
        for row in range(GROUP):
            pick[n, row, 16 * (row // ROWS) + row % ROWS + ROWS * n] = 1.0
    bf = jnp.bfloat16
    return pl.pallas_call(
        refresh_kernel,
        out_shape=(jax.ShapeDtypeStruct((FEAT, 4 * SUB), bf),) * 2 + (jax.ShapeDtypeStruct((4 * SUB, FEAT), bf),),
        in_specs=[VMEM] * 3 + [ANY] * 6,
        out_specs=(ANY, ANY, ANY),
        scratch_shapes=[
            pltpu.VMEM((16, RUN), jnp.float32),
            pltpu.VMEM((2, 2, 16, RUN), bf),
            pltpu.VMEM((16, 16, RUN), bf),
            pltpu.VMEM((2, TOKENS, WIDE), bf),
            pltpu.VMEM((WIDE, 4 * SUB), bf),
            pltpu.VMEM((2 * SUB, WIDE), bf),
            pltpu.VMEM((TOKENS, 4 * SUB), bf),
            pltpu.VMEM((TOKENS, 2 * SUB), bf),
            pltpu.VMEM((NZ, OWN, 4 * SUB), bf),
            pltpu.VMEM((NZ, OWN, 2 * SUB), bf),
            pltpu.VMEM((TOKENS, SUB), bf),
            pltpu.VMEM((TOKENS, 2 * SUB), bf),
            pltpu.VMEM((WIDE, 2 * SUB), bf),
            pltpu.VMEM((SUB, WIDE), bf),
            DMA((15,)), DMA((15,)),
            DMA((3, 6)), DMA((3, 6)), DMA((6,)),
            DMA((2, 2, 3)), DMA((2, 2, 3)),
            DMA((2, 2, 4, 3)), DMA((2, 2, 4, 3)),
            DMA((2, 4, 4)), DMA((2, 4, 4)),
            DMA((2, NZ)), DMA((2, NZ)), DMA((2, NZ)), DMA((2, NZ)),
            DMA((3, 3)), DMA((3, 3)), DMA((3,)),
        ],
        compiler_params=pltpu.CompilerParams(
            collective_id=0, has_side_effects=True, vmem_limit_bytes=60 << 20
        ),
    )(tokens, cotangent, jnp.asarray(pick, bf), gate, up, pgate, pup, down, pdown)


def sophia_update(hess_prev, probe, product, moment):
    new_hess = decay_rate * hess_prev + (1.0 - decay_rate) * probe.astype(jnp.float32) * product.astype(jnp.float32)
    ratio = moment.astype(jnp.float32) / jnp.maximum(curvature_scale * new_hess, floor_value)
    return new_hess, jnp.clip(ratio, -1.0, 1.0).astype(jnp.bfloat16)


def local(
    tokens, cotangent, gate_weight, up_weight, down_weight, probe_gate, probe_up, probe_down,
    hess_gate, hess_up, hess_down, moment_gate, moment_up, moment_down,
):
    products = products_of(
        tokens, cotangent, gate_weight, up_weight, probe_gate, probe_up, down_weight, probe_down
    )
    new_hess_gate, step_gate = sophia_update(hess_gate, probe_gate, products[0], moment_gate)
    new_hess_up, step_up = sophia_update(hess_up, probe_up, products[1], moment_up)
    new_hess_down, step_down = sophia_update(hess_down, probe_down, products[2], moment_down)
    return new_hess_gate, new_hess_up, new_hess_down, step_gate, step_up, step_down


def solution(mesh):
    cols, rows, split = P("tensor", "dp"), P("dp", "tensor"), P(("dp", "tensor"), None)
    per = (cols, cols, rows)
    return jax.shard_map(
        local, mesh=mesh,
        in_specs=(split, split) + per * 4,
        out_specs=per * 2,
        check_vma=False,
    )
```

```python
import jax
import jax.numpy as jnp
import numpy as np
from jax import lax
from jax.experimental import pallas as pl
from jax.experimental.pallas import tpu as pltpu
from jax.sharding import PartitionSpec as P

decay_rate = 0.9
curvature_scale = 0.05
floor_value = 0.01

MESH = pl.DeviceIdType.MESH
ANY = pl.BlockSpec(memory_space=pl.ANY)
VMEM = pl.BlockSpec(memory_space=pltpu.VMEM)
DMA = pltpu.SemaphoreType.DMA

NX, NY, NZ = 4, 4, 4
ROWS = 5
GROUP = 80
FEAT = 512
WIDE = NY * FEAT
TOKENS = 1280
SUB = 128


def place():
    d = lax.axis_index("dp")
    t = lax.axis_index("tensor")
    return d // 8, t // 2, (d // 2) % 4, t % 2, d % 2


def device(x, y, zh, zl, c):
    return {"dp": x * 8 + zh * 2 + c, "tensor": y * 2 + zl}


def remote(src, dst, send, recv, target):
    return pltpu.make_async_remote_copy(
        src_ref=src, dst_ref=dst, send_sem=send, recv_sem=recv,
        device_id=target, device_id_type=MESH,
    )

LANE = WIDE // 2
HALF = LANE // 2
RUN = 384
SPAN = TOKENS // NZ
OWN = SPAN // 2
ZREL = (0, 3, 1, 2)
TOK, COT = 0, 1


def refresh_kernel(
    tok_ref, cot_ref, pick_ref, gate_ref, up_ref, pgate_ref, pup_ref, down_ref, pdown_ref,
    hess_g, hess_u, hess_d, mom_g, mom_u, mom_d,
    gate_out, up_out, down_out, hess_g_out, hess_u_out, hess_d_out, prb_g_out, prb_u_out, prb_d_out,
    mom_g_out, mom_u_out, mom_d_out,
    packed32, packed, pieces, every, wide, tall, part_t, part_c, far_t, far_c, tan_h, tan_gu, back_wide, back_tall,
    ps, pr, ws, wr, wl, zs, zr, xs, xr, ss, sr, rs, rr, ts, tr, os, orr, ol, near_sem,
):
    x, y, zh, zl, c = place()
    f32, bf = jnp.float32, jnp.bfloat16
    group = [(dc, dy, dz) for dc in range(2) for dy in range(4) for dz in range(2)][1:]
    mates = [((y + dy) % 4, zl ^ dz, c ^ dc) for dc, dy, dz in group]
    sib = device(x, y, zh, zl, 1 - c)
    pair = device(x, y, zh, 1 - zl, c)
    zn, zp = device(x, y, (zh + 1) % 4, zl, c), device(x, y, (zh + 3) % 4, zl, c)
    xn, xp = device((x + 1) % 4, y, zh, zl, c), device((x + 3) % 4, y, zh, zl, c)
    held = []
    for k, (src, dst) in enumerate((
        (hess_g, hess_g_out), (hess_u, hess_u_out), (hess_d, hess_d_out),
        (pgate_ref, prb_g_out), (pup_ref, prb_u_out), (pdown_ref, prb_d_out),
        (mom_g, mom_g_out), (mom_u, mom_u_out), (mom_d, mom_d_out),
    )):
        held.append(pltpu.make_async_copy(src, dst, near_sem.at[k]))
    barrier = pltpu.get_barrier_semaphore()
    friends = [device(x, my, zh, mz, mc) for my, mz, mc in mates] + [zn, zp, xn, xp]
    for friend in friends:
        pl.semaphore_signal(barrier, inc=1, device_id=friend, device_id_type=MESH)

    packed32[...] = jnp.zeros_like(packed32)

    def pack(arr):
        for mz in range(2):
            for mc in range(2):
                for n in range(8):
                    col = ((2 * mc + n // 4) * 2 + mz) * FEAT + n % 4 * SUB
                    row, at = n // 3 * ROWS, n % 3 * SUB
                    packed32[row:row + ROWS, at:at + SUB] = (tok_ref, cot_ref)[arr][:, col:col + SUB].astype(f32)
                packed[arr, mz, mc] = packed32[...].astype(bf)

    me = c * 8 + y * 2 + zl
    piece_copies = ([], [])

    def scatter(arr):
        for k, (my, mz, mc) in enumerate(mates):
            cp = remote(
                packed.at[arr, mz, mc], pieces.at[arr, me], ps.at[arr, k], pr.at[arr, k],
                device(x, my, zh, mz, mc),
            )
            cp.start()
            piece_copies[arr].append(cp)
        pieces[arr, me] = packed[arr, zl, c]

    def merge(arr):
        for cp in piece_copies[arr]:
            cp.wait_recv()
        spread = pieces[arr].reshape(256, RUN)
        where(arr, 0, 0)[...] = jnp.concatenate([
            jnp.dot(pick_ref[n], spread[:, :min(RUN, LANE - n * RUN)], preferred_element_type=f32).astype(bf)
            for n in range(3)
        ], axis=1)

    pack(TOK)
    pl.semaphore_wait(barrier, len(friends))
    scatter(TOK)
    pack(COT)
    scatter(COT)

    weight_copies = []
    col_refs = (gate_ref, up_ref, pgate_ref, pup_ref)
    row_refs = (down_ref, pdown_ref)

    def cut(k, to):
        if k < 4:
            return (
                col_refs[k].at[:, pl.ds(pl.multiple_of(to * SUB, SUB), SUB)],
                wide.at[pl.ds(pl.multiple_of(y * FEAT, FEAT), FEAT), pl.ds(k * SUB, SUB)],
            )
        return (
            row_refs[k - 4].at[pl.ds(pl.multiple_of(to * SUB, SUB), SUB), :],
            tall.at[pl.ds((k - 4) * SUB, SUB), pl.ds(pl.multiple_of(y * FEAT, FEAT), FEAT)],
        )

    def lend(kinds):
        for k in kinds:
            for dy in (1, 3, 2):
                to = (y + dy) % 4
                src, dst = cut(k, to)
                cp = remote(src, dst, ws.at[dy - 1, k], wr.at[dy - 1, k], device(x, to, zh, zl, c))
                cp.start()
                weight_copies.append(cp)
            src, dst = cut(k, y)
            cp = pltpu.make_async_copy(src, dst, wl.at[k])
            cp.start()
            weight_copies.append(cp)

    sends = []

    def where(arr, dx, k, half=None):
        g = ((zh + ZREL[k]) % 4) * 4 + (x + dx) % 4
        rows = pl.ds(pl.multiple_of(g * GROUP, 16), GROUP)
        if half is None:
            return every.at[arr, rows, pl.ds(pl.multiple_of(c * LANE, LANE), LANE)]
        return every.at[arr, rows, pl.ds(pl.multiple_of(c * LANE + half * HALF, HALF), HALF)]

    def go(src, dst, s, r, target):
        cp = remote(src, dst, s, r, target)
        cp.start()
        sends.append(cp)

    def arrive(dst, s, r):
        remote(dst, dst, s, r, sib).wait_recv()

    def share(a, dx, k):
        ref = where(a, dx, k)
        go(ref, ref, ss.at[a, dx, k], sr.at[a, dx, k], sib)

    def shared(a, k):
        for dx in range(4):
            g = ((zh + ZREL[k]) % 4) * 4 + (x + dx) % 4
            rows = pl.ds(pl.multiple_of(g * GROUP, 16), GROUP)
            ref = every.at[a, rows, pl.ds(pl.multiple_of((1 - c) * LANE, LANE), LANE)]
            arrive(ref, ss.at[a, dx, k], sr.at[a, dx, k])

    def z_send(a, way, half):
        ref = where(a, 0, 0, half)
        cp = remote(ref, ref, zs.at[a, way, half], zr.at[a, way, half], (zn, zp)[way])
        cp.start()
        return cp

    def z_get(a, way, half):
        ref = where(a, 0, 1 + way, half)
        arrive(ref, zs.at[a, way, half], zr.at[a, way, half])
        if half == way:
            go(ref, ref, zs.at[a, way, 2], zr.at[a, way, 2], (zn, zp)[way])
        x_send(a, 1 + way, half)

    def z_end(a):
        for way in range(2):
            arrive(where(a, 0, 3, way), zs.at[a, way, 2], zr.at[a, way, 2])
            x_send(a, 3, way)
        share(a, 0, 3)

    def x_send(a, k, half):
        ref = where(a, 0, k, half)
        for way in (half, 1 - half):
            go(ref, ref, xs.at[a, way, k, half], xr.at[a, way, k, half], (xn, xp)[way])

    def x_get(a, way, k, half):
        ref = where(a, (3, 1)[way], k, half)
        arrive(ref, xs.at[a, way, k, half], xr.at[a, way, k, half])
        if half == way:
            go(ref, ref, xs.at[a, way, k, 2], xr.at[a, way, k, 2], (xn, xp)[way])

    def x_share(a, k):
        share(a, 3, k)
        share(a, 1, k)

    def x_end(a, k):
        for way in range(2):
            arrive(where(a, 2, k, way), xs.at[a, way, k, 2], xr.at[a, way, k, 2])
        share(a, 2, k)

    def span(k):
        return ((zh + ZREL[k]) % 4) * SPAN

    def rows_of(k):
        return pl.ds(pl.multiple_of(span(k), 16), SPAN)

    def near(k):
        return pl.ds(pl.multiple_of(span(k) + zl * OWN, 16), OWN)

    def away(k):
        return pl.ds(pl.multiple_of(span(k) + (1 - zl) * OWN, 16), OWN)

    def sum_t(k):
        shared(TOK, k)
        part_t[rows_of(k), :] = jnp.dot(every[TOK, rows_of(k), :], wide[...], preferred_element_type=f32).astype(bf)
        go(part_t.at[away(k), :], far_t.at[k], rs.at[0, k], rr.at[0, k], pair)

    def sum_c(k):
        shared(COT, k)
        part_c[rows_of(k), :] = lax.dot_general(
            every[COT, rows_of(k), :], tall[...], (((1,), (1,)), ((), ())), preferred_element_type=f32
        ).astype(bf)
        go(part_c.at[away(k), :], far_c.at[k], rs.at[1, k], rr.at[1, k], pair)

    def total_t(k, n):
        cols = slice(n * SUB, (n + 1) * SUB)
        return part_t[near(k), cols].astype(f32) + far_t[k, :, cols].astype(f32)

    def total_c(k, n):
        cols = slice(n * SUB, (n + 1) * SUB)
        return part_c[near(k), cols].astype(f32) + far_c[k, :, cols].astype(f32)

    def hidden(k):
        arrive(far_t.at[k], rs.at[0, k], rr.at[0, k])
        gate_pre, up_pre, gate_tan, up_tan = (total_t(k, n) for n in range(4))
        logistic = 1.0 / (1.0 + jnp.exp(-gate_pre))
        first = logistic * (1.0 + gate_pre * (1.0 - logistic))
        tan_h[near(k), :] = (first * gate_tan * up_pre + gate_pre * logistic * up_tan).astype(bf)
        ref = tan_h.at[near(k), :]
        go(ref, ref, ts.at[0, k], tr.at[0, k], pair)

    def tangent(k):
        arrive(far_c.at[k], rs.at[1, k], rr.at[1, k])
        gate_pre, up_pre, gate_tan, up_tan = (total_t(k, n) for n in range(4))
        back, back_tan = (total_c(k, n) for n in range(2))
        logistic = 1.0 / (1.0 + jnp.exp(-gate_pre))
        first = logistic * (1.0 + gate_pre * (1.0 - logistic))
        second = logistic * (1.0 - logistic) * (2.0 + gate_pre * (1.0 - 2.0 * logistic))
        tan_gu[near(k), 0:SUB] = (
            back_tan * up_pre * first + back * up_tan * first + back * up_pre * second * gate_tan
        ).astype(bf)
        tan_gu[near(k), SUB:] = (back_tan * gate_pre * logistic + back * first * gate_tan).astype(bf)
        ref = tan_gu.at[near(k), :]
        go(ref, ref, ts.at[1, k], tr.at[1, k], pair)

    def there(ref, n, k):
        ref = ref.at[away(k), :]
        arrive(ref, ts.at[n, k], tr.at[n, k])

    out_copies = []
    mine = pl.ds(pl.multiple_of(y * SUB, SUB), SUB)

    def give(dy, pairs):
        to = (y + dy) % 4
        for k, src, dst in pairs:
            if dy:
                cp = remote(src, dst, os.at[dy - 1, k], orr.at[dy - 1, k], device(x, to, zh, zl, c))
            else:
                cp = pltpu.make_async_copy(src, dst, ol.at[k])
            cp.start()
            out_copies.append(cp)

    def feats_of(dy):
        return pl.ds(pl.multiple_of(((y + dy) % 4) * FEAT, FEAT), FEAT)

    def product_down(dy):
        feats = feats_of(dy)
        back_tall[:, feats] = (lax.dot_general(
            tan_h[...], every[COT, :, feats], (((0,), (0,)), ((), ())), preferred_element_type=f32
        ) * (1.0 / TOKENS)).astype(bf)
        give(dy, [(2, back_tall.at[:, feats], down_out.at[mine, :])])

    def product_wide(dy):
        feats = feats_of(dy)
        both = lax.dot_general(
            tan_gu[...], every[TOK, :, feats], (((0,), (0,)), ((), ())), preferred_element_type=f32
        ) * (1.0 / TOKENS)
        back_wide[feats, :] = both.T.astype(bf)
        give(dy, [
            (0, back_wide.at[feats, pl.ds(0, SUB)], gate_out.at[:, mine]),
            (1, back_wide.at[feats, pl.ds(SUB, SUB)], up_out.at[:, mine]),
        ])

    lend(range(4))
    for cp in held:
        cp.start()
    merge(TOK)
    t_first = [z_send(TOK, 0, 0), z_send(TOK, 1, 1)]
    x_send(TOK, 0, 0)
    x_send(TOK, 0, 1)
    share(TOK, 0, 0)
    merge(COT)
    for cp in t_first:
        cp.wait_send()
    sends.append(z_send(TOK, 0, 1))
    sends.append(z_send(TOK, 1, 0))
    x_send(COT, 0, 0)
    x_send(COT, 0, 1)
    share(COT, 0, 0)
    x_get(TOK, 0, 0, 0)
    x_get(TOK, 1, 0, 1)
    z_get(TOK, 0, 0)
    z_get(TOK, 1, 1)
    c_first = [z_send(COT, 0, 0), z_send(COT, 1, 1)]
    x_get(TOK, 0, 0, 1)
    x_get(TOK, 1, 0, 0)
    x_share(TOK, 0)
    z_get(TOK, 0, 1)
    z_get(TOK, 1, 0)
    share(TOK, 0, 1)
    share(TOK, 0, 2)
    x_end(TOK, 0)
    z_end(TOK)
    lend((4, 5))
    for cp in c_first:
        cp.wait_send()
    sends.append(z_send(COT, 0, 1))
    sends.append(z_send(COT, 1, 0))
    x_get(COT, 0, 0, 0)
    x_get(COT, 1, 0, 1)
    x_get(TOK, 0, 1, 0)
    x_get(TOK, 1, 2, 1)
    x_get(TOK, 1, 1, 1)
    x_get(TOK, 0, 2, 0)
    z_get(COT, 0, 0)
    z_get(COT, 1, 1)
    x_get(TOK, 1, 1, 0)
    x_get(TOK, 0, 2, 1)
    x_get(TOK, 0, 1, 1)
    x_get(TOK, 1, 2, 0)
    x_share(TOK, 1)
    x_share(TOK, 2)
    x_get(COT, 0, 0, 1)
    x_get(COT, 1, 0, 0)
    x_share(COT, 0)
    z_get(COT, 0, 1)
    z_get(COT, 1, 0)
    share(COT, 0, 1)
    share(COT, 0, 2)
    for cp in weight_copies[:16]:
        cp.wait()
    sum_t(0)
    x_get(TOK, 0, 3, 0)
    x_get(TOK, 1, 3, 1)
    x_end(TOK, 1)
    x_end(TOK, 2)
    x_get(TOK, 0, 3, 1)
    x_get(TOK, 1, 3, 0)
    x_share(TOK, 3)
    z_end(COT)
    sum_t(1)
    x_end(COT, 0)
    x_get(COT, 0, 1, 0)
    x_get(COT, 1, 2, 1)
    sum_t(2)
    x_end(TOK, 3)
    x_get(COT, 1, 1, 1)
    x_get(COT, 0, 2, 0)
    sum_t(3)
    x_get(COT, 1, 1, 0)
    x_get(COT, 0, 2, 1)
    x_get(COT, 0, 1, 1)
    x_get(COT, 1, 2, 0)
    x_share(COT, 1)
    x_share(COT, 2)
    for cp in weight_copies[16:]:
        cp.wait()
    sum_c(0)
    x_get(COT, 0, 3, 0)
    x_get(COT, 1, 3, 1)
    x_end(COT, 1)
    x_end(COT, 2)
    sum_c(1)
    sum_c(2)
    x_get(COT, 0, 3, 1)
    x_get(COT, 1, 3, 0)
    x_share(COT, 3)
    for k in range(4):
        hidden(k)
    x_end(COT, 3)
    tangent(0)
    sum_c(3)
    tangent(1)
    tangent(2)
    for k in range(4):
        there(tan_h, 0, k)
    product_down(2)
    product_down(1)
    product_down(3)
    tangent(3)
    product_down(0)
    for k in range(4):
        there(tan_gu, 1, k)
    for dy in (2, 1, 3, 0):
        product_wide(dy)
    for cp in held:
        cp.wait()
    for cp in out_copies:
        cp.wait()
    for arr in (TOK, COT):
        for cp in piece_copies[arr]:
            cp.wait_send()
    for cp in sends:
        cp.wait_send()


def products_of(tokens, cotangent, gate, up, pgate, pup, down, pdown, *state):
    pick = np.zeros((3, GROUP, 256), np.float32)
    for n in range(3):
        for row in range(GROUP):
            pick[n, row, 16 * (row // ROWS) + row % ROWS + ROWS * n] = 1.0
    bf = jnp.bfloat16
    return pl.pallas_call(
        refresh_kernel,
        out_shape=tuple(pltpu.VMEM((FEAT, FEAT), t) for t in (bf,) * 3 + (jnp.float32,) * 3 + (bf,) * 6),
        in_specs=[VMEM] * 3 + [ANY] * 12,
        out_specs=(VMEM,) * 12,
        scratch_shapes=[
            pltpu.VMEM((16, RUN), jnp.float32),
            pltpu.VMEM((2, 2, 2, 16, RUN), bf),
            pltpu.VMEM((2, 16, 16, RUN), bf),
            pltpu.VMEM((2, TOKENS, WIDE), bf),
            pltpu.VMEM((WIDE, 4 * SUB), bf),
            pltpu.VMEM((2 * SUB, WIDE), bf),
            pltpu.VMEM((TOKENS, 4 * SUB), bf),
            pltpu.VMEM((TOKENS, 2 * SUB), bf),
            pltpu.VMEM((NZ, OWN, 4 * SUB), bf),
            pltpu.VMEM((NZ, OWN, 2 * SUB), bf),
            pltpu.VMEM((TOKENS, SUB), bf),
            pltpu.VMEM((TOKENS, 2 * SUB), bf),
            pltpu.VMEM((WIDE, 2 * SUB), bf),
            pltpu.VMEM((SUB, WIDE), bf),
            DMA((2, 15)), DMA((2, 15)),
            DMA((3, 6)), DMA((3, 6)), DMA((6,)),
            DMA((2, 2, 3)), DMA((2, 2, 3)),
            DMA((2, 2, 4, 3)), DMA((2, 2, 4, 3)),
            DMA((2, 4, 4)), DMA((2, 4, 4)),
            DMA((2, NZ)), DMA((2, NZ)), DMA((2, NZ)), DMA((2, NZ)),
            DMA((3, 3)), DMA((3, 3)), DMA((3,)), DMA((9,)),
        ],
        compiler_params=pltpu.CompilerParams(
            collective_id=0, has_side_effects=True, vmem_limit_bytes=111 << 19
        ),
    )(tokens, cotangent, jnp.asarray(pick, bf), gate, up, pgate, pup, down, pdown, *state)


def sophia_update(hess_prev, probe, product, moment):
    new_hess = decay_rate * hess_prev + (1.0 - decay_rate) * probe.astype(jnp.float32) * product.astype(jnp.float32)
    ratio = moment.astype(jnp.float32) / jnp.maximum(curvature_scale * new_hess, floor_value)
    return new_hess, jnp.clip(ratio, -1.0, 1.0).astype(jnp.bfloat16)


def local(
    tokens, cotangent, gate_weight, up_weight, down_weight, probe_gate, probe_up, probe_down,
    hess_gate, hess_up, hess_down, moment_gate, moment_up, moment_down,
):
    held = products_of(
        tokens, cotangent, gate_weight, up_weight, probe_gate, probe_up, down_weight, probe_down,
        hess_gate, hess_up, hess_down, moment_gate, moment_up, moment_down,
    )
    products, hess, probes, moments = held[:3], held[3:6], held[6:9], held[9:]
    new_hess_gate, step_gate = sophia_update(hess[0], probes[0], products[0], moments[0])
    new_hess_up, step_up = sophia_update(hess[1], probes[1], products[1], moments[1])
    new_hess_down, step_down = sophia_update(hess[2], probes[2], products[2], moments[2])
    return new_hess_gate, new_hess_up, new_hess_down, step_gate, step_up, step_down


def solution(mesh):
    cols, rows, split = P("tensor", "dp"), P("dp", "tensor"), P(("dp", "tensor"), None)
    per = (cols, cols, rows)
    return jax.shard_map(
        local, mesh=mesh,
        in_specs=(split, split) + per * 4,
        out_specs=per * 2,
        check_vma=False,
    )
```

```python
import jax
import jax.numpy as jnp
import numpy as np
from jax import lax
from jax.experimental import pallas as pl
from jax.experimental.pallas import tpu as pltpu
from jax.sharding import PartitionSpec as P

decay_rate = 0.9
curvature_scale = 0.05
floor_value = 0.01

MESH = pl.DeviceIdType.MESH
ANY = pl.BlockSpec(memory_space=pl.ANY)
VMEM = pl.BlockSpec(memory_space=pltpu.VMEM)
DMA = pltpu.SemaphoreType.DMA

NX, NY, NZ = 4, 4, 4
ROWS = 5
GROUP = 80
FEAT = 512
WIDE = NY * FEAT
TOKENS = 1280
SUB = 128


def place():
    d = lax.axis_index("dp")
    t = lax.axis_index("tensor")
    return d // 8, t // 2, (d // 2) % 4, t % 2, d % 2


def device(x, y, zh, zl, c):
    return {"dp": x * 8 + zh * 2 + c, "tensor": y * 2 + zl}


def remote(src, dst, send, recv, target):
    return pltpu.make_async_remote_copy(
        src_ref=src, dst_ref=dst, send_sem=send, recv_sem=recv,
        device_id=target, device_id_type=MESH,
    )

LANE = WIDE // 2
HALF = LANE // 2
RUN = 384
SPAN = TOKENS // NZ
OWN = SPAN // 2
ZREL = (0, 3, 1, 2)
TOK, COT = 0, 1


def refresh_kernel(
    tok_ref, cot_ref, pick_ref, gate_ref, up_ref, pgate_ref, pup_ref, down_ref, pdown_ref,
    hess_g, hess_u, hess_d, mom_g, mom_u, mom_d,
    gate_out, up_out, down_out, hess_g_out, hess_u_out, hess_d_out, prb_g_out, prb_u_out, prb_d_out,
    mom_g_out, mom_u_out, mom_d_out,
    packed32, packed, pieces, every, wide, tall, part_t, part_c, far_t, far_c, tan_h, tan_gu, back_wide, back_tall,
    ps, pr, ws, wr, wl, zs, zr, xs, xr, ss, sr, rs, rr, ts, tr, os, orr, ol, near_sem,
):
    x, y, zh, zl, c = place()
    f32, bf = jnp.float32, jnp.bfloat16
    group = [(dc, dy, dz) for dc in range(2) for dy in range(4) for dz in range(2)][1:]
    mates = [((y + dy) % 4, zl ^ dz, c ^ dc) for dc, dy, dz in group]
    sib = device(x, y, zh, zl, 1 - c)
    pair = device(x, y, zh, 1 - zl, c)
    zn, zp = device(x, y, (zh + 1) % 4, zl, c), device(x, y, (zh + 3) % 4, zl, c)
    xn, xp = device((x + 1) % 4, y, zh, zl, c), device((x + 3) % 4, y, zh, zl, c)
    held = []
    for k, (src, dst) in enumerate((
        (hess_g, hess_g_out), (hess_u, hess_u_out), (hess_d, hess_d_out),
        (pgate_ref, prb_g_out), (pup_ref, prb_u_out), (pdown_ref, prb_d_out),
        (mom_g, mom_g_out), (mom_u, mom_u_out), (mom_d, mom_d_out),
    )):
        held.append(pltpu.make_async_copy(src, dst, near_sem.at[k]))
    barrier = pltpu.get_barrier_semaphore()
    friends = [device(x, my, zh, mz, mc) for my, mz, mc in mates] + [zn, zp, xn, xp]
    for friend in friends:
        pl.semaphore_signal(barrier, inc=1, device_id=friend, device_id_type=MESH)

    packed32[...] = jnp.zeros_like(packed32)

    def pack(arr):
        for mz in range(2):
            for mc in range(2):
                for n in range(8):
                    col = ((2 * mc + n // 4) * 2 + mz) * FEAT + n % 4 * SUB
                    row, at = n // 3 * ROWS, n % 3 * SUB
                    packed32[row:row + ROWS, at:at + SUB] = (tok_ref, cot_ref)[arr][:, col:col + SUB].astype(f32)
                packed[arr, mz, mc] = packed32[...].astype(bf)

    me = c * 8 + y * 2 + zl
    piece_copies = ([], [])

    def scatter(arr):
        for k, (my, mz, mc) in enumerate(mates):
            cp = remote(
                packed.at[arr, mz, mc], pieces.at[arr, me], ps.at[arr, k], pr.at[arr, k],
                device(x, my, zh, mz, mc),
            )
            cp.start()
            piece_copies[arr].append(cp)
        pieces[arr, me] = packed[arr, zl, c]

    def merge(arr):
        for cp in piece_copies[arr]:
            cp.wait_recv()
        spread = pieces[arr].reshape(256, RUN)
        where(arr, 0, 0)[...] = jnp.concatenate([
            jnp.dot(pick_ref[n], spread[:, :min(RUN, LANE - n * RUN)], preferred_element_type=f32).astype(bf)
            for n in range(3)
        ], axis=1)

    pack(TOK)
    pl.semaphore_wait(barrier, len(friends))
    scatter(TOK)
    pack(COT)
    scatter(COT)

    weight_copies = []
    col_refs = (gate_ref, up_ref, pgate_ref, pup_ref)
    row_refs = (down_ref, pdown_ref)

    def cut(k, to):
        if k < 4:
            return (
                col_refs[k].at[:, pl.ds(pl.multiple_of(to * SUB, SUB), SUB)],
                wide.at[pl.ds(pl.multiple_of(y * FEAT, FEAT), FEAT), pl.ds(k * SUB, SUB)],
            )
        return (
            row_refs[k - 4].at[pl.ds(pl.multiple_of(to * SUB, SUB), SUB), :],
            tall.at[pl.ds((k - 4) * SUB, SUB), pl.ds(pl.multiple_of(y * FEAT, FEAT), FEAT)],
        )

    def lend(kinds):
        for k in kinds:
            for dy in (1, 3, 2):
                to = (y + dy) % 4
                src, dst = cut(k, to)
                cp = remote(src, dst, ws.at[dy - 1, k], wr.at[dy - 1, k], device(x, to, zh, zl, c))
                cp.start()
                weight_copies.append(cp)
            src, dst = cut(k, y)
            cp = pltpu.make_async_copy(src, dst, wl.at[k])
            cp.start()
            weight_copies.append(cp)

    sends = []

    def where(arr, dx, k, half=None):
        g = ((zh + ZREL[k]) % 4) * 4 + (x + dx) % 4
        rows = pl.ds(pl.multiple_of(g * GROUP, 16), GROUP)
        if half is None:
            return every.at[arr, rows, pl.ds(pl.multiple_of(c * LANE, LANE), LANE)]
        return every.at[arr, rows, pl.ds(pl.multiple_of(c * LANE + half * HALF, HALF), HALF)]

    def go(src, dst, s, r, target):
        cp = remote(src, dst, s, r, target)
        cp.start()
        sends.append(cp)

    def arrive(dst, s, r):
        remote(dst, dst, s, r, sib).wait_recv()

    def share(a, dx, k):
        ref = where(a, dx, k)
        go(ref, ref, ss.at[a, dx, k], sr.at[a, dx, k], sib)

    def shared(a, k):
        for dx in range(4):
            g = ((zh + ZREL[k]) % 4) * 4 + (x + dx) % 4
            rows = pl.ds(pl.multiple_of(g * GROUP, 16), GROUP)
            ref = every.at[a, rows, pl.ds(pl.multiple_of((1 - c) * LANE, LANE), LANE)]
            arrive(ref, ss.at[a, dx, k], sr.at[a, dx, k])

    def z_send(a, way, half):
        ref = where(a, 0, 0, half)
        cp = remote(ref, ref, zs.at[a, way, half], zr.at[a, way, half], (zn, zp)[way])
        cp.start()
        return cp

    def z_get(a, way, half):
        ref = where(a, 0, 1 + way, half)
        arrive(ref, zs.at[a, way, half], zr.at[a, way, half])
        if half == way:
            go(ref, ref, zs.at[a, way, 2], zr.at[a, way, 2], (zn, zp)[way])
        x_send(a, 1 + way, half)

    def z_end(a):
        for way in range(2):
            arrive(where(a, 0, 3, way), zs.at[a, way, 2], zr.at[a, way, 2])
            x_send(a, 3, way)
        share(a, 0, 3)

    def x_send(a, k, half):
        ref = where(a, 0, k, half)
        for way in (half, 1 - half):
            go(ref, ref, xs.at[a, way, k, half], xr.at[a, way, k, half], (xn, xp)[way])

    def x_get(a, way, k, half):
        ref = where(a, (3, 1)[way], k, half)
        arrive(ref, xs.at[a, way, k, half], xr.at[a, way, k, half])
        if half == way:
            go(ref, ref, xs.at[a, way, k, 2], xr.at[a, way, k, 2], (xn, xp)[way])

    def x_share(a, k):
        share(a, 3, k)
        share(a, 1, k)

    def x_end(a, k):
        for way in range(2):
            arrive(where(a, 2, k, way), xs.at[a, way, k, 2], xr.at[a, way, k, 2])
        share(a, 2, k)

    def span(k):
        return ((zh + ZREL[k]) % 4) * SPAN

    def rows_of(k):
        return pl.ds(pl.multiple_of(span(k), 16), SPAN)

    def near(k):
        return pl.ds(pl.multiple_of(span(k) + zl * OWN, 16), OWN)

    def away(k):
        return pl.ds(pl.multiple_of(span(k) + (1 - zl) * OWN, 16), OWN)

    def sum_t(k):
        shared(TOK, k)
        part_t[rows_of(k), :] = jnp.dot(every[TOK, rows_of(k), :], wide[...], preferred_element_type=f32).astype(bf)
        go(part_t.at[away(k), :], far_t.at[k], rs.at[0, k], rr.at[0, k], pair)

    def sum_c(k):
        shared(COT, k)
        part_c[rows_of(k), :] = lax.dot_general(
            every[COT, rows_of(k), :], tall[...], (((1,), (1,)), ((), ())), preferred_element_type=f32
        ).astype(bf)
        go(part_c.at[away(k), :], far_c.at[k], rs.at[1, k], rr.at[1, k], pair)

    def total_t(k, n):
        cols = slice(n * SUB, (n + 1) * SUB)
        return part_t[near(k), cols].astype(f32) + far_t[k, :, cols].astype(f32)

    def total_c(k, n):
        cols = slice(n * SUB, (n + 1) * SUB)
        return part_c[near(k), cols].astype(f32) + far_c[k, :, cols].astype(f32)

    def hidden(k):
        arrive(far_t.at[k], rs.at[0, k], rr.at[0, k])
        gate_pre, up_pre, gate_tan, up_tan = (total_t(k, n) for n in range(4))
        logistic = 1.0 / (1.0 + jnp.exp(-gate_pre))
        first = logistic * (1.0 + gate_pre * (1.0 - logistic))
        tan_h[near(k), :] = (first * gate_tan * up_pre + gate_pre * logistic * up_tan).astype(bf)
        ref = tan_h.at[near(k), :]
        go(ref, ref, ts.at[0, k], tr.at[0, k], pair)

    def tangent(k):
        arrive(far_c.at[k], rs.at[1, k], rr.at[1, k])
        gate_pre, up_pre, gate_tan, up_tan = (total_t(k, n) for n in range(4))
        back, back_tan = (total_c(k, n) for n in range(2))
        logistic = 1.0 / (1.0 + jnp.exp(-gate_pre))
        first = logistic * (1.0 + gate_pre * (1.0 - logistic))
        second = logistic * (1.0 - logistic) * (2.0 + gate_pre * (1.0 - 2.0 * logistic))
        tan_gu[near(k), 0:SUB] = (
            back_tan * up_pre * first + back * up_tan * first + back * up_pre * second * gate_tan
        ).astype(bf)
        tan_gu[near(k), SUB:] = (back_tan * gate_pre * logistic + back * first * gate_tan).astype(bf)
        ref = tan_gu.at[near(k), :]
        go(ref, ref, ts.at[1, k], tr.at[1, k], pair)

    def there(ref, n, k):
        ref = ref.at[away(k), :]
        arrive(ref, ts.at[n, k], tr.at[n, k])

    out_copies = []
    mine = pl.ds(pl.multiple_of(y * SUB, SUB), SUB)

    def give(dy, pairs):
        to = (y + dy) % 4
        for k, src, dst in pairs:
            if dy:
                cp = remote(src, dst, os.at[dy - 1, k], orr.at[dy - 1, k], device(x, to, zh, zl, c))
            else:
                cp = pltpu.make_async_copy(src, dst, ol.at[k])
            cp.start()
            out_copies.append(cp)

    def feats_of(dy):
        return pl.ds(pl.multiple_of(((y + dy) % 4) * FEAT, FEAT), FEAT)

    def product_down(dy):
        feats = feats_of(dy)
        back_tall[:, feats] = (lax.dot_general(
            tan_h[...], every[COT, :, feats], (((0,), (0,)), ((), ())), preferred_element_type=f32
        ) * (1.0 / TOKENS)).astype(bf)
        give(dy, [(2, back_tall.at[:, feats], down_out.at[mine, :])])

    def product_wide(dy):
        feats = feats_of(dy)
        both = lax.dot_general(
            tan_gu[...], every[TOK, :, feats], (((0,), (0,)), ((), ())), preferred_element_type=f32
        ) * (1.0 / TOKENS)
        back_wide[feats, :] = both.T.astype(bf)
        give(dy, [
            (0, back_wide.at[feats, pl.ds(0, SUB)], gate_out.at[:, mine]),
            (1, back_wide.at[feats, pl.ds(SUB, SUB)], up_out.at[:, mine]),
        ])

    lend(range(4))
    for cp in held:
        cp.start()
    merge(TOK)
    t_first = [z_send(TOK, 0, 0), z_send(TOK, 1, 1)]
    x_send(TOK, 0, 0)
    x_send(TOK, 0, 1)
    share(TOK, 0, 0)
    merge(COT)
    for cp in t_first:
        cp.wait_send()
    sends.append(z_send(TOK, 0, 1))
    sends.append(z_send(TOK, 1, 0))
    x_send(COT, 0, 0)
    x_send(COT, 0, 1)
    share(COT, 0, 0)
    x_get(TOK, 0, 0, 0)
    x_get(TOK, 1, 0, 1)
    z_get(TOK, 0, 0)
    z_get(TOK, 1, 1)
    c_first = [z_send(COT, 0, 0), z_send(COT, 1, 1)]
    x_get(TOK, 0, 0, 1)
    x_get(TOK, 1, 0, 0)
    x_share(TOK, 0)
    z_get(TOK, 0, 1)
    z_get(TOK, 1, 0)
    share(TOK, 0, 1)
    share(TOK, 0, 2)
    x_end(TOK, 0)
    z_end(TOK)
    lend((4, 5))
    for cp in c_first:
        cp.wait_send()
    sends.append(z_send(COT, 0, 1))
    sends.append(z_send(COT, 1, 0))
    x_get(COT, 0, 0, 0)
    x_get(COT, 1, 0, 1)
    x_get(TOK, 0, 1, 0)
    x_get(TOK, 1, 2, 1)
    x_get(TOK, 1, 1, 1)
    x_get(TOK, 0, 2, 0)
    z_get(COT, 0, 0)
    z_get(COT, 1, 1)
    x_get(TOK, 1, 1, 0)
    x_get(TOK, 0, 2, 1)
    x_get(TOK, 0, 1, 1)
    x_get(TOK, 1, 2, 0)
    x_share(TOK, 1)
    x_share(TOK, 2)
    x_get(COT, 0, 0, 1)
    x_get(COT, 1, 0, 0)
    x_share(COT, 0)
    z_get(COT, 0, 1)
    z_get(COT, 1, 0)
    share(COT, 0, 1)
    share(COT, 0, 2)
    for cp in weight_copies[:16]:
        cp.wait()
    sum_t(0)
    x_get(TOK, 0, 3, 0)
    x_get(TOK, 1, 3, 1)
    x_end(TOK, 1)
    x_end(TOK, 2)
    x_get(TOK, 0, 3, 1)
    x_get(TOK, 1, 3, 0)
    x_share(TOK, 3)
    z_end(COT)
    sum_t(1)
    x_end(COT, 0)
    x_get(COT, 0, 1, 0)
    x_get(COT, 1, 2, 1)
    sum_t(2)
    x_end(TOK, 3)
    x_get(COT, 1, 1, 1)
    x_get(COT, 0, 2, 0)
    sum_t(3)
    x_get(COT, 1, 1, 0)
    x_get(COT, 0, 2, 1)
    x_get(COT, 0, 1, 1)
    x_get(COT, 1, 2, 0)
    x_share(COT, 1)
    x_share(COT, 2)
    for cp in weight_copies[16:]:
        cp.wait()
    sum_c(0)
    x_get(COT, 0, 3, 0)
    x_get(COT, 1, 3, 1)
    hidden(0)
    hidden(1)
    x_end(COT, 1)
    x_end(COT, 2)
    sum_c(1)
    sum_c(2)
    x_get(COT, 0, 3, 1)
    x_get(COT, 1, 3, 0)
    x_share(COT, 3)
    hidden(2)
    hidden(3)
    tangent(0)
    x_end(COT, 3)
    sum_c(3)
    tangent(1)
    tangent(2)
    for k in range(4):
        there(tan_h, 0, k)
    product_down(2)
    product_down(1)
    product_down(3)
    tangent(3)
    product_down(0)
    for k in range(4):
        there(tan_gu, 1, k)
    for dy in (2, 1, 3, 0):
        product_wide(dy)
    for arr in (TOK, COT):
        for cp in piece_copies[arr]:
            cp.wait_send()
    for cp in sends:
        cp.wait_send()
    for cp in held:
        cp.wait()
    for cp in out_copies:
        cp.wait()


def products_of(tokens, cotangent, gate, up, pgate, pup, down, pdown, *state):
    pick = np.zeros((3, GROUP, 256), np.float32)
    for n in range(3):
        for row in range(GROUP):
            pick[n, row, 16 * (row // ROWS) + row % ROWS + ROWS * n] = 1.0
    bf = jnp.bfloat16
    return pl.pallas_call(
        refresh_kernel,
        out_shape=tuple(pltpu.VMEM((FEAT, FEAT), t) for t in (bf,) * 3 + (jnp.float32,) * 3 + (bf,) * 6),
        in_specs=[VMEM] * 3 + [ANY] * 12,
        out_specs=(VMEM,) * 12,
        scratch_shapes=[
            pltpu.VMEM((16, RUN), jnp.float32),
            pltpu.VMEM((2, 2, 2, 16, RUN), bf),
            pltpu.VMEM((2, 16, 16, RUN), bf),
            pltpu.VMEM((2, TOKENS, WIDE), bf),
            pltpu.VMEM((WIDE, 4 * SUB), bf),
            pltpu.VMEM((2 * SUB, WIDE), bf),
            pltpu.VMEM((TOKENS, 4 * SUB), bf),
            pltpu.VMEM((TOKENS, 2 * SUB), bf),
            pltpu.VMEM((NZ, OWN, 4 * SUB), bf),
            pltpu.VMEM((NZ, OWN, 2 * SUB), bf),
            pltpu.VMEM((TOKENS, SUB), bf),
            pltpu.VMEM((TOKENS, 2 * SUB), bf),
            pltpu.VMEM((WIDE, 2 * SUB), bf),
            pltpu.VMEM((SUB, WIDE), bf),
            DMA((2, 15)), DMA((2, 15)),
            DMA((3, 6)), DMA((3, 6)), DMA((6,)),
            DMA((2, 2, 3)), DMA((2, 2, 3)),
            DMA((2, 2, 4, 3)), DMA((2, 2, 4, 3)),
            DMA((2, 4, 4)), DMA((2, 4, 4)),
            DMA((2, NZ)), DMA((2, NZ)), DMA((2, NZ)), DMA((2, NZ)),
            DMA((3, 3)), DMA((3, 3)), DMA((3,)), DMA((9,)),
        ],
        compiler_params=pltpu.CompilerParams(
            collective_id=0, has_side_effects=True, vmem_limit_bytes=111 << 19
        ),
    )(tokens, cotangent, jnp.asarray(pick, bf), gate, up, pgate, pup, down, pdown, *state)


def sophia_update(hess_prev, probe, product, moment):
    new_hess = decay_rate * hess_prev + (1.0 - decay_rate) * probe.astype(jnp.float32) * product.astype(jnp.float32)
    ratio = moment.astype(jnp.float32) / jnp.maximum(curvature_scale * new_hess, floor_value)
    return new_hess, jnp.clip(ratio, -1.0, 1.0).astype(jnp.bfloat16)


def local(
    tokens, cotangent, gate_weight, up_weight, down_weight, probe_gate, probe_up, probe_down,
    hess_gate, hess_up, hess_down, moment_gate, moment_up, moment_down,
):
    held = products_of(
        tokens, cotangent, gate_weight, up_weight, probe_gate, probe_up, down_weight, probe_down,
        hess_gate, hess_up, hess_down, moment_gate, moment_up, moment_down,
    )
    products, hess, probes, moments = held[:3], held[3:6], held[6:9], held[9:]
    new_hess_gate, step_gate = sophia_update(hess[0], probes[0], products[0], moments[0])
    new_hess_up, step_up = sophia_update(hess[1], probes[1], products[1], moments[1])
    new_hess_down, step_down = sophia_update(hess[2], probes[2], products[2], moments[2])
    return new_hess_gate, new_hess_up, new_hess_down, step_gate, step_up, step_down


def solution(mesh):
    cols, rows, split = P("tensor", "dp"), P("dp", "tensor"), P(("dp", "tensor"), None)
    per = (cols, cols, rows)
    return jax.shard_map(
        local, mesh=mesh,
        in_specs=(split, split) + per * 4,
        out_specs=per * 2,
        check_vma=False,
    )
```
